256 devices in a mesh: ctx: 32 (over z, x_lo, core), head: 8 (over x_hi, y).
Axes of the slice: x: 4 (x_hi: 2, x_lo: 2; x = x_hi * 2 + x_lo), y: 4, z: 8, core: 2. Of those that a mesh axis runs over, the one named last changes fastest.
Arguments:
- query: bfloat16 [8192, 8, 128], P('ctx', 'head'), may hold values from -8 to 8
- key: bfloat16 [8192, 128], P('ctx'), may hold values from -8 to 8
- value: bfloat16 [8192, 128], P('ctx'), may hold values from -6 to 6
- grad_out: bfloat16 [8192, 8, 128], P('ctx', 'head'), may hold values from -96 to 96
- doc_ids: int32 [8192], replicated, may hold values from 0 to 7, never falling along the last dimension, each value on 1 to 4096 neighbouring positions
- tile_mask: int32 [64, 64], replicated, may hold values from 0 to 1, as said below
Outputs:
- grad_query: bfloat16 [8192, 8, 128], P('ctx', 'head')
- grad_key: bfloat16 [8192, 128], P('ctx')
- grad_value: bfloat16 [8192, 128], P('ctx')
The draws below stay inside these ranges and needn't reach their ends.
Inputs may be any that keep to these rules, and one draw needn't show every extreme that they name: `tile_mask`: tiles on the diagonal are 1.
All inputs are finite; a program needn't handle non-finite values.
Results may differ from the reference program's by a relative error of at most 0.011.
Values may be sent and summed in bfloat16 or wider, within the bound.
A program may use at most 64 MiB of HBM per device.

```python
import math
import jax
import jax.numpy as jnp
import numpy as np
from jax import lax

DH = 128
HQ = 8
TILE = 128
DOCS = 8
SEQ = 8192
NB = 64
N_CTX = 32


def draw_query(key, part):
    key = jax.random.fold_in(key, 11)
    base = jnp.clip(jax.random.normal(key, (SEQ, HQ, DH), jnp.float32), -6.0, 6.0)
    return base.astype(jnp.bfloat16)


def draw_key(key, part):
    key = jax.random.fold_in(key, 23)
    base = jnp.clip(jax.random.normal(key, (SEQ, DH), jnp.float32), -6.0, 6.0)
    return base.astype(jnp.bfloat16)


def draw_tile_mask(key, part):
    key = jax.random.fold_in(key, 7)
    bits = jax.random.randint(key, (NB, NB), 0, 2)
    diagonal = (jnp.arange(NB)[:, None] == jnp.arange(NB)[None, :]).astype(jnp.int32)
    return jnp.maximum(bits, diagonal).astype(jnp.int32)


def shard_levels(own_key, dims, cuts, smallest, high):
    level, own = 1.0, jax.random.fold_in(own_key, 6)
    for dim, shards_of in cuts:
        heights = jnp.exp(jax.random.uniform(jax.random.fold_in(own, dim), (shards_of,), jnp.float32, smallest / len(cuts), high / len(cuts)))
        level = level * jnp.repeat(heights, dims[dim] // shards_of).reshape([-1 if axis == dim else 1 for axis in range(len(dims))])
    return level


def length_profile(amount, total, limit, slope):
    portions = [(1 << 20) // math.isqrt(rank ** slope) + 1 for rank in range(2, amount + 1)]
    rest, given = total - limit - (amount - 1), [1] * (amount - 1)
    while rest > 0:
        movable = [i for i in range(amount - 1) if given[i] < limit]
        mass, remaining = sum([portions[i] for i in movable]), rest
        for i in movable:
            extra = min(limit - given[i], max(1, remaining * portions[i] // mass), rest)
            given[i] = given[i] + extra
            rest = rest - extra
    return np.array([limit] + given)


def uneven_parts(key, amount, total, most, skew):
    if amount == 2:
        one = jax.random.randint(key, (), max(1, total - most), min(most, total - 1) + 1)
        return jnp.stack([one, total - one])
    tallies = jnp.asarray(length_profile(amount, total, most, skew), jnp.int32)
    couples = (amount - 1) // 2
    donor, sink = tallies[1:1 + 2 * couples:2], tallies[2:2 + 2 * couples:2]
    margin = jnp.minimum(donor - 1, most - sink)
    moved = jax.random.randint(jax.random.fold_in(key, 1), (couples,), 0, 1 << 20) % (margin + 1)
    tallies = tallies.at[1:1 + 2 * couples:2].set(donor - moved).at[2:2 + 2 * couples:2].set(sink + moved)
    return tallies[jax.random.permutation(jax.random.fold_in(key, 2), amount)]


def centred(stream_key, shape, spread, reach, cuts=(), kind=jnp.bfloat16):
    entries = spread * jax.random.normal(stream_key, shape, jnp.float32)
    if cuts:
        entries = entries * shard_levels(stream_key, shape, cuts, -0.22, 0.18)
    return jnp.clip(entries, -reach, reach).astype(kind)


def setup_inputs(seed: int = 0) -> dict:
    arg_keys = jax.random.split(jax.random.key(seed), 7)
    query = draw_query(jax.random.fold_in(arg_keys[6], 71), 0)
    key = draw_key(jax.random.fold_in(arg_keys[6], 71), 0)
    value = centred(arg_keys[2], (SEQ, DH), 1.0, 6.0, ((0, 32),))
    grad_out = centred(arg_keys[3], (SEQ, HQ, DH), 16.0, 96.0, ((0, 32), (1, 8)))
    doc_ids = jnp.searchsorted(jnp.cumsum(uneven_parts(arg_keys[4], DOCS, SEQ, SEQ // 2, 0)), jnp.arange(SEQ), side="right").astype(jnp.int32)
    tile_mask = draw_tile_mask(jax.random.fold_in(arg_keys[6], 71), 0)
    return {"query": query, "key": key, "value": value, "grad_out": grad_out, "doc_ids": doc_ids, "tile_mask": tile_mask}


NEG_LARGE = -1e30


def stored_order(values, pieces):
    half_rows = values.shape[0] // (2 * pieces)
    blocks = values.reshape(2 * pieces, half_rows)
    paired = jnp.concatenate([blocks[:pieces], blocks[pieces:][::-1]], axis=1)
    return paired.reshape(values.shape[0])


def reference(query, key, value, grad_out, doc_ids, tile_mask):
    seq_len = key.shape[0]
    score_scale = DH ** -0.5
    positions = stored_order(jnp.arange(seq_len, dtype=jnp.int32), N_CTX)
    documents = stored_order(doc_ids, N_CTX)
    tiles = (positions // TILE).astype(jnp.int32)
    block_rows = math.gcd(seq_len, 512)
    block_count = seq_len // block_rows

    def head_pass(running, head_index):
        query_head = lax.dynamic_index_in_dim(query, head_index, 1, keepdims=False)
        grad_head = lax.dynamic_index_in_dim(grad_out, head_index, 1, keepdims=False)

        def row_pass(sums, block_index):
            key_sum, value_sum = sums
            first_row = (block_index * block_rows).astype(jnp.int32)
            query_rows = lax.dynamic_slice_in_dim(query_head, first_row, block_rows, 0)
            grad_rows = lax.dynamic_slice_in_dim(grad_head, first_row, block_rows, 0)
            query_pos = lax.dynamic_slice_in_dim(positions, first_row, block_rows, 0)
            query_doc = lax.dynamic_slice_in_dim(documents, first_row, block_rows, 0)
            query_tile = lax.dynamic_slice_in_dim(tiles, first_row, block_rows, 0)
            allowed = (positions[None, :] <= query_pos[:, None]) & (documents[None, :] == query_doc[:, None])
            allowed = allowed & (tile_mask[query_tile[:, None], tiles[None, :]] == 1)
            scores = jnp.dot(query_rows, key.T, preferred_element_type=jnp.float32) * score_scale
            masked = jnp.where(allowed, scores, NEG_LARGE)
            row_max = jnp.max(masked, axis=1, keepdims=True)
            log_total = row_max + jnp.log(jnp.sum(jnp.exp(masked - row_max), axis=1, keepdims=True))
            probabilities = jnp.where(allowed, jnp.exp(masked - log_total), 0.0)
            weights_b = probabilities.astype(jnp.bfloat16)
            attended = jnp.dot(weights_b, value, preferred_element_type=jnp.float32)
            row_delta = jnp.sum(grad_rows.astype(jnp.float32) * attended, axis=1, keepdims=True)
            grad_probs = jnp.dot(grad_rows, value.T, preferred_element_type=jnp.float32)
            grad_scores = (probabilities * (grad_probs - row_delta)).astype(jnp.bfloat16)
            query_grad = (score_scale * jnp.dot(grad_scores, key, preferred_element_type=jnp.float32)).astype(jnp.bfloat16)
            key_sum = key_sum + score_scale * jnp.dot(grad_scores.T, query_rows, preferred_element_type=jnp.float32)
            value_sum = value_sum + jnp.dot(weights_b.T, grad_rows, preferred_element_type=jnp.float32)
            return (key_sum, value_sum), query_grad

        running, query_blocks = lax.scan(row_pass, running, jnp.arange(block_count, dtype=jnp.int32))
        return running, query_blocks.reshape(seq_len, DH)

    empty_sum = jnp.zeros((seq_len, DH), jnp.float32)
    (key_sum, value_sum), query_grads = lax.scan(head_pass, (empty_sum, empty_sum), jnp.arange(HQ, dtype=jnp.int32))
    grad_query = jnp.transpose(query_grads, (1, 0, 2))
    return grad_query, key_sum.astype(jnp.bfloat16), value_sum.astype(jnp.bfloat16)
```

```python
import functools

import jax
import jax.numpy as jnp
from jax import lax
from jax.experimental import pallas as pl
from jax.experimental.pallas import tpu as pltpu
from jax.sharding import PartitionSpec as P

MESH = pl.DeviceIdType.MESH
BF, F32 = jnp.bfloat16, jnp.float32
SCALE = 128 ** -0.5
SCALE_2 = SCALE * 1.4426950408889634
CLOSED = -131072.0
TILES_MOD, DOC_AT, LOW_AT, HIGH_AT = 48, 48, 56, 88


def dot_nt(a, b):
    return lax.dot_general(a, b, (((1,), (1,)), ((), ())), preferred_element_type=F32)


def dot_nn(a, b):
    return lax.dot_general(a, b, (((1,), (0,)), ((), ())), preferred_element_type=F32)


def dot_tn(a, b):
    return lax.dot_general(a, b, (((0,), (0,)), ((), ())), preferred_element_type=F32)


def kernel(
    q_ref, do_ref, k_ref, v_ref, doc_ref, tm_ref,
    gq_ref, gk_ref, gv_ref,
    kv, kf, qd, qf, doc_in, tm_in, doc_t, tm_row, sc, dp, mx, st, st_in, acc, dq_t,
    sq, rq, sd, rd, sx, rx, sz, rz, fin,
    i_s, z_s, z_r, y_s, y_r, x_s, x_r, c_s, c_r, st_s, st_r, q_s, q_r,
    d_s, d_r, xx_s, xx_r, zz_s, zz_r, h_s, h_r,
):
    ctx, head = lax.axis_index("ctx"), lax.axis_index("head")
    z, w = ctx // 4, ctx % 4
    x_lo, core = w // 2, w % 2
    x_hi, y = head // 4, head % 4
    x = 2 * x_hi + x_lo

    def device(zt, xt, yt, ct):
        return (zt * 4 + (xt % 2) * 2 + ct, (xt // 2) * 4 + yt)

    z_dev = lambda k: device((z + k) % 8, x, y, core)
    x_dev = lambda k: device(z, (x + k) % 4, y, core)
    y_dev = lambda k: device(z, x, (y + k) % 4, core)
    c_dev = device(z, x, y, 1 - core)
    h_dev = lambda k: (ctx, (head + k) % 8)

    def remote(src, dst, s, r, to):
        return pltpu.make_async_remote_copy(
            src_ref=src, dst_ref=dst, send_sem=s, recv_sem=r, device_id=to, device_id_type=MESH
        )

    barrier = pltpu.get_barrier_semaphore()
    peers = [z_dev(k) for k in range(1, 8)] + [x_dev(k) for k in range(1, 4)] + [c_dev]
    peers += [h_dev(k) for k in range(1, 8)]
    for peer in peers:
        pl.semaphore_signal(barrier, inc=1, device_id=peer, device_id_type=MESH)

    own_rows = pl.multiple_of(y * 32 + x_hi * 16, 16)

    def rows_of(xs, cs):
        return pl.ds(pl.multiple_of(((xs % 2) * 2 + cs) * 32 + (xs // 2) * 16, 16), 16)

    my_rows = rows_of(x, core)
    loads = []
    for high in (0, 1):
        theirs = pl.ds(own_rows + 128 * high, 16)
        loads.append((v_ref.at[theirs, :], kv.at[z, high, my_rows, pl.ds(0, 128)]))
        loads.append((k_ref.at[theirs, :], kv.at[z, high, my_rows, pl.ds(128, 128)]))
    for high in (0, 1):
        theirs = pl.ds(128 * high, 128)
        loads.append((do_ref.at[theirs, :], qd.at[high, y, :, pl.ds(0, 128)]))
        loads.append((q_ref.at[theirs, :], qd.at[high, y, :, pl.ds(128, 128)]))
    loads += [(doc_ref, doc_in), (tm_ref, tm_in)]
    loads = [pltpu.make_async_copy(a, b, i_s.at[n]) for n, (a, b) in enumerate(loads)]
    for load in loads:
        load.start()

    def clear(n, carry):
        acc[n, 0] = jnp.zeros((128, 256), F32)
        acc[n, 1] = jnp.zeros((128, 256), F32)
        return carry

    lax.fori_loop(0, 8, clear, 0)
    mx[...] = jnp.full((2, 8, 512), -3e38, F32)
    for load in loads[8:]:
        load.wait()

    doc_t[...] = jnp.concatenate([doc_in[...].astype(F32), jnp.zeros((64, 128), F32)], axis=0).T
    low_tile, high_tile = ctx, 63 - ctx
    lane32 = lax.broadcasted_iota(jnp.int32, (32, 128), 1)
    sub32 = lax.broadcasted_iota(jnp.int32, (32, 128), 0)
    doc_lane = (lane32 >= DOC_AT) & (lane32 < DOC_AT + 8)
    doc_of_lane = (lane32 - DOC_AT).astype(F32)

    docs_mine = doc_t[pl.ds(pl.multiple_of(y * 32, 32), 32), :]

    def key_features(t, carry):
        doc = jnp.sum(jnp.where(lane32 == t, docs_mine, 0.0), axis=1, keepdims=True)
        hit = (lane32 == t % TILES_MOD) | (doc_lane & (doc != doc_of_lane))
        low_lane = sub32 + jnp.where(t == low_tile, LOW_AT, 1000)
        high_lane = sub32 + jnp.where(t == high_tile, HIGH_AT, 1000)
        hit = hit | (lane32 == low_lane) | (lane32 == high_lane)
        high = t // 32
        at = jnp.where(high == 1, 63 - t, t)
        rows = pl.ds(pl.multiple_of((at % 4) * 32, 32), 32)
        kf[at // 4, high, rows, :] = jnp.where(hit, 1.0, 0.0).astype(BF)
        return carry

    lax.fori_loop(0, 64, key_features, 0, unroll=8)

    def query_features():
        lane = lax.broadcasted_iota(jnp.int32, (128, 128), 1)
        sub = lax.broadcasted_iota(jnp.int32, (128, 128), 0)
        for high in (0, 1):
            tile = high_tile if high else low_tile
            first = 28 - 4 * z if high else 0
            causal_at = HIGH_AT if high else LOW_AT
            doc = jnp.sum(jnp.where(lane == tile, doc_t[...], 0.0), axis=1, keepdims=True)
            tm_row[...] = jnp.zeros((8, 128), F32)
            tm_row[:, 0:64] = jnp.broadcast_to(tm_in[pl.ds(tile, 1), :].astype(F32), (8, 64))
            row = tm_row[...]
            row_far = pltpu.roll(row, 128 - TILES_MOD, 1)
            lane8 = lax.broadcasted_iota(jnp.int32, (8, 128), 1)
            near = lane8 >= first
            tile_at = jnp.where(near, lane8, lane8 + TILES_MOD)
            is_open = (jnp.where(near, row, row_far) > 0.5) & (tile_at <= tile)
            closed = jnp.where((lane8 < TILES_MOD) & jnp.logical_not(is_open), 1.0, 0.0)[0:1, :]
            hit = jnp.broadcast_to(closed, (128, 128)) > 0.5
            own_doc = doc == (lane - DOC_AT).astype(F32)
            hit = hit | ((lane >= DOC_AT) & (lane < DOC_AT + 8) & own_doc)
            later = (lane >= causal_at) & (lane < causal_at + 32) & (y * 32 + lane - causal_at > sub)
            qf[high] = jnp.where(hit | later, CLOSED, 0.0).astype(BF)

    query_features()
    for load in loads[:8]:
        load.wait()
    pl.semaphore_wait(barrier, len(peers))

    def piece(k, j, cs):
        return kv.at[(z + k) % 8, :, rows_of((x + 4 - j) % 4, cs), :]

    def z_copy(k):
        mine = piece(0, 0, core)
        return remote(mine, mine, z_s.at[k], z_r.at[k], z_dev(k))

    def x_copy(j, k):
        mine = piece(k, 0, core)
        return remote(mine, mine, x_s.at[j, k], x_r.at[j, k], x_dev(j))

    def c_copy(j, cs):
        theirs = kv.at[:, :, rows_of((x + 4 - j) % 4, cs), :]
        return remote(theirs, theirs, c_s.at[j], c_r.at[j], c_dev)

    for k in (4, 3, 5, 2, 6, 1, 7):
        z_copy(k).start()
    y_copies = []
    for k in (2, 1, 3):
        mine = qd.at[:, y]
        copy = remote(mine, mine, y_s.at[k], y_r.at[k], y_dev(k))
        copy.start()
        y_copies.append(copy)

    for k in (0, 1, 7, 2, 6, 3, 5, 4):
        if k:
            theirs = piece(8 - k, 0, core)
            remote(theirs, theirs, z_s.at[k], z_r.at[k], z_dev(k)).wait_recv()
        for j in (2, 1, 3):
            x_copy(j, (8 - k) % 8).start()
    c_copy(0, core).start()
    for j in (1, 3, 2):
        for k in (0, 7, 1, 6, 2, 5, 3, 4):
            theirs = piece(k, j, core)
            remote(theirs, theirs, x_s.at[j, k], x_r.at[j, k], x_dev(j)).wait_recv()
        c_copy(j, core).start()

    def send_waits():
        for k in range(8):
            if k:
                z_copy(k).wait_send()
            for j in (1, 2, 3):
                x_copy(j, k).wait_send()
        for j in range(4):
            c_copy(j, core).wait_send()

    for copy in y_copies:
        copy.wait()
    for j in range(4):
        c_copy(j, 1 - core).wait_recv()

    def query_rows(high):
        return jnp.concatenate([qd[high, a, :, 128:256] for a in range(4)], axis=0)

    def out_rows(high):
        return jnp.concatenate([qd[high, a, :, 0:128] for a in range(4)], axis=0)

    def low_chunk(i):
        return i, 0, 16 + i

    def high_chunk(i):
        near = i <= z
        plane = jnp.where(near, 7 - z + i, i - 1)
        return plane, jnp.where(near, 0, 1), jnp.where(near, plane, 8 + plane)

    chunk_of = (low_chunk, high_chunk)
    counts, groups = ((z + 2) // 2, 3), (2, 3)

    for high in (1, 0):

        group = groups[high]

        def scores(i, largest):
            chunks = [chunk_of[high](i * group + g) for g in range(group)]
            queries = jnp.concatenate(
                [query_rows(high), jnp.concatenate([qf[high]] * 4, axis=0)], axis=1
            )
            keys = [
                jnp.concatenate([kv[n, part, :, 128:256], kf[n, part]], axis=1)
                for n, part, slot in chunks
            ]
            values = [kv[n, part, :, 0:128] for n, part, slot in chunks]
            s = dot_nt(jnp.concatenate(keys, axis=0), queries)
            d = dot_nt(jnp.concatenate(values, axis=0), out_rows(high))
            for g, (n, part, slot) in enumerate(chunks):
                sc[slot] = s[128 * g : 128 * g + 128]
                dp[slot] = d[128 * g : 128 * g + 128]
            return jnp.maximum(largest, jnp.max(s.reshape(16 * group, 8, 512), axis=0))

        largest = lax.fori_loop(0, counts[high], scores, mx[high])
        largest = jnp.max(largest, axis=0, keepdims=True) * SCALE_2

        def sums(i, carry):
            total, delta = carry
            totals, deltas = [0.0] * 4, [0.0] * 4
            for g in range(group):
                slot = chunk_of[high](i * group + g)[2]
                for a in range(4):
                    cols = slice(128 * a, 128 * a + 128)
                    e = jnp.exp2(sc[slot, :, cols] * SCALE_2 - largest[:, cols])
                    sc[slot, :, cols] = e
                    totals[a] += jnp.sum(e.reshape(16, 8, 128), axis=0)
                    deltas[a] += jnp.sum((e * dp[slot, :, cols]).reshape(16, 8, 128), axis=0)
            return (
                total + jnp.concatenate(totals, axis=1),
                delta + jnp.concatenate(deltas, axis=1),
            )

        zero = jnp.zeros((8, 512), F32)
        total, delta = lax.fori_loop(0, counts[high], sums, (zero, zero))
        total = jnp.sum(total, axis=0, keepdims=True)
        delta = jnp.sum(delta, axis=0, keepdims=True)
        for a in range(4):
            cols = slice(128 * a, 128 * a + 128)
            st[high, a : a + 1, :] = largest[:, cols]
            st[high, 4 + a : 5 + a, :] = total[:, cols]
            st[high, 8 + a : 9 + a, :] = delta[:, cols]
        st[high, 12:16, :] = jnp.zeros((4, 128), F32)
        for k in (2, 1, 3):
            remote(
                st.at[high], st_in.at[k, high], st_s.at[high, k], st_r.at[high, k], y_dev(k)
            ).start()

    def row_stats(high):
        for k in (1, 3, 2):
            remote(
                st.at[high], st_in.at[k, high], st_s.at[high, k], st_r.at[high, k], y_dev(k)
            ).wait()
        parts = [st[high]] + [st_in[k, high] for k in (1, 2, 3)]
        most = functools.reduce(jnp.maximum, [p[0:4, :] for p in parts])
        weights = [jnp.exp2(p[0:4, :] - most) for p in parts]
        total = sum(wt * p[4:8, :] for wt, p in zip(weights, parts))
        delta = sum(wt * p[8:12, :] for wt, p in zip(weights, parts)) / total
        return weights[0] / total, delta

    def grads_of(high, factor, delta):
        def grads(i, carry):
            n, part, slot = chunk_of[high](i)
            probs, grad_s = [], []
            for a in range(4):
                cols = slice(128 * a, 128 * a + 128)
                p = sc[slot, :, cols] * factor[a : a + 1, :]
                probs.append(p.astype(BF))
                grad_s.append((p * (dp[slot, :, cols] - delta[a : a + 1, :])).astype(BF))
            probs, grad_s = jnp.concatenate(probs, axis=1), jnp.concatenate(grad_s, axis=1)
            acc[n, part, :, 0:128] += dot_nn(probs, out_rows(high))
            acc[n, part, :, 128:256] += dot_nn(grad_s, query_rows(high))
            dq_t[high] += dot_tn(kv[n, part, :, 128:256], grad_s)
            return carry

        return grads

    def d_copy(part):
        return remote(sd.at[part], rd.at[part], d_s.at[part], d_r.at[part], c_dev)

    def split(part):
        def step(n, carry):
            for h in (0, 1):
                rows = pl.ds(pl.multiple_of((2 * h + 1 - core) * 32, 32), 32)
                sd[part, n, h] = acc[n, part, rows, :].astype(BF)
            return carry

        lax.fori_loop(0, 8, step, 0)
        d_copy(part).start()

    def xx_copy(part, k):
        return remote(
            sx.at[part, (x + k) % 4], rx.at[part, k], xx_s.at[part, k], xx_r.at[part, k], x_dev(k)
        )

    def sum_cores(part):
        d_copy(part).wait()

        def step(n, carry):
            for h in (0, 1):
                rows = pl.ds(pl.multiple_of((2 * h + core) * 32, 32), 32)
                both = (acc[n, part, rows, :] + rd[part, n, h].astype(F32)).astype(BF)
                sx[part, h, n] = both[0:16]
                sx[part, 2 + h, n] = both[16:32]
            return carry

        lax.fori_loop(0, 8, step, 0)
        for k in (2, 1, 3):
            xx_copy(part, k).start()

    def zz_copy(part, k):
        return remote(
            sz.at[part, (z + k) % 8], rz.at[part, k], zz_s.at[part, k], zz_r.at[part, k], z_dev(k)
        )

    def sum_x(part):
        for k in (1, 3, 2):
            xx_copy(part, k).wait()

        def step(n, carry):
            total = sx[part, x, n].astype(F32) + sum(rx[part, k, n].astype(F32) for k in (1, 2, 3))
            sz[part, n] = total.astype(BF)
            return carry

        lax.fori_loop(0, 8, step, 0)
        for k in (4, 3, 5, 2, 6, 1, 7):
            zz_copy(part, k).start()

    def h_copy(part, k):
        mine = fin.at[part, pl.ds(own_rows, 16), :]
        return remote(mine, mine, h_s.at[part, k], h_r.at[part, k], h_dev(k))

    def sum_z(part):
        for k in (1, 7, 2, 6, 3, 5, 4):
            zz_copy(part, k).wait()
        total = sz[part, z].astype(F32) + sum(rz[part, k].astype(F32) for k in range(1, 8))
        total = jnp.concatenate([total[:, 0:128], total[:, 128:256] * SCALE], axis=1)
        fin[part, pl.ds(own_rows, 16), :] = total.astype(BF)
        for k in (6, 2, 4, 1, 3, 5, 7):
            h_copy(part, k).start()

    def gathered(part):
        for k in (4, 1, 7, 3, 5, 2, 6):
            sender = (head + 8 - k) % 8
            rows = pl.multiple_of((sender % 4) * 32 + (sender // 4) * 16, 16)
            theirs = fin.at[part, pl.ds(rows, 16), :]
            remote(theirs, theirs, h_s.at[part, k], h_r.at[part, k], h_dev(k)).wait_recv()
        gv_ref[128 * part : 128 * part + 128, :] = fin[part, :, 0:128]
        gk_ref[128 * part : 128 * part + 128, :] = fin[part, :, 128:256]

    dq_t[...] = jnp.zeros((2, 128, 512), F32)
    factor, delta = row_stats(1)
    grads = grads_of(1, factor, delta)
    lax.fori_loop(z + 1, 9, grads, 0)
    split(1)
    lax.fori_loop(0, z + 1, grads, 0)
    factor, delta = row_stats(0)
    sum_cores(1)
    grads = grads_of(0, factor, delta)
    lax.fori_loop(0, z + 1, grads, 0)
    split(0)

    for a in range(4):
        for high in (0, 1):
            rows = slice(128 * high, 128 * high + 128)
            sq[a, rows, :] = dq_t[high, :, 128 * a : 128 * a + 128].T.astype(BF)
    q_copies = []
    for k in (2, 1, 3):
        copy = remote(sq.at[(y + k) % 4], rq.at[k], q_s.at[k], q_r.at[k], y_dev(k))
        copy.start()
        q_copies.append(copy)
    sum_cores(0)
    sum_x(1)
    send_waits()
    for copy in q_copies:
        copy.wait()
    total = sq[y].astype(F32) + sum(rq[k].astype(F32) for k in (1, 2, 3))
    gq_ref[...] = (SCALE * total).astype(BF)
    sum_x(0)
    sum_z(1)
    sum_z(0)
    gathered(1)
    gathered(0)
    for part in (1, 0):
        for k in range(1, 8):
            h_copy(part, k).wait_send()


def body(query, key, value, grad_out, doc_ids, tile_mask):
    vmem = pl.BlockSpec(memory_space=pltpu.VMEM)
    hbm = pl.BlockSpec(memory_space=pltpu.HBM)
    dma = lambda *shape: pltpu.SemaphoreType.DMA(shape)
    scratch = [
        pltpu.VMEM((8, 2, 128, 256), BF),
        pltpu.VMEM((8, 2, 128, 128), BF),
        pltpu.VMEM((2, 4, 128, 256), BF),
        pltpu.VMEM((2, 128, 128), BF),
        pltpu.VMEM((64, 128), jnp.int32),
        pltpu.VMEM((64, 64), jnp.int32),
        pltpu.VMEM((128, 128), F32),
        pltpu.VMEM((8, 128), F32),
        pltpu.VMEM((24, 128, 512), F32),
        pltpu.VMEM((24, 128, 512), F32),
        pltpu.VMEM((2, 8, 512), F32),
        pltpu.VMEM((2, 16, 128), F32),
        pltpu.VMEM((4, 2, 16, 128), F32),
        pltpu.VMEM((8, 2, 128, 256), F32),
        pltpu.VMEM((2, 128, 512), F32),
        pltpu.VMEM((4, 256, 128), BF),
        pltpu.VMEM((4, 256, 128), BF),
        pltpu.VMEM((2, 8, 2, 32, 256), BF),
        pltpu.VMEM((2, 8, 2, 32, 256), BF),
        pltpu.VMEM((2, 4, 8, 16, 256), BF),
        pltpu.VMEM((2, 4, 8, 16, 256), BF),
        pltpu.VMEM((2, 8, 16, 256), BF),
        pltpu.VMEM((2, 8, 16, 256), BF),
        pltpu.VMEM((2, 128, 256), BF),
        dma(10), dma(8), dma(8), dma(4), dma(4), dma(4, 8), dma(4, 8), dma(4), dma(4),
        dma(2, 4), dma(2, 4), dma(4), dma(4),
        dma(2), dma(2), dma(2, 4), dma(2, 4), dma(2, 8), dma(2, 8), dma(2, 8), dma(2, 8),
    ]
    grad_query, grad_key, grad_value = pl.pallas_call(
        kernel,
        out_shape=[jax.ShapeDtypeStruct((256, 128), BF)] * 3,
        in_specs=[hbm] * 6,
        out_specs=[vmem] * 3,
        scratch_shapes=scratch,
        compiler_params=pltpu.CompilerParams(
            collective_id=0, has_side_effects=True, vmem_limit_bytes=56 << 20
        ),
        cost_estimate=pl.CostEstimate(flops=3 << 30, bytes_accessed=1 << 20, transcendentals=1 << 20),
        name="attention_grads",
    )(
        query.reshape(256, 128),
        grad_out.reshape(256, 128),
        key,
        value,
        doc_ids.reshape(64, 128),
        tile_mask,
    )
    return grad_query.reshape(256, 1, 128), grad_key, grad_value


def solution(mesh):
    rows, heads = P("ctx", None), P("ctx", "head", None)
    return jax.shard_map(
        body,
        mesh=mesh,
        in_specs=(heads, rows, rows, heads, P(), P()),
        out_specs=(heads, rows, rows),
        check_vma=False,
    )
```

```python
import functools

import jax
import jax.numpy as jnp
from jax import lax
from jax.experimental import pallas as pl
from jax.experimental.pallas import tpu as pltpu
from jax.sharding import PartitionSpec as P

MESH = pl.DeviceIdType.MESH
BF, F32 = jnp.bfloat16, jnp.float32
SCALE = 128 ** -0.5
SCALE_2 = SCALE * 1.4426950408889634
CLOSED = -131072.0
TILES_MOD, DOC_AT, LOW_AT, HIGH_AT = 48, 48, 56, 88


def dot_nt(a, b):
    return lax.dot_general(a, b, (((1,), (1,)), ((), ())), preferred_element_type=F32)


def dot_nn(a, b):
    return lax.dot_general(a, b, (((1,), (0,)), ((), ())), preferred_element_type=F32)


def dot_tn(a, b):
    return lax.dot_general(a, b, (((0,), (0,)), ((), ())), preferred_element_type=F32)


def kernel(
    q_ref, do_ref, k_ref, v_ref, doc_ref, tm_ref,
    gq_ref, gk_ref, gv_ref,
    kv, kf, qd, qf, doc_in, tm_in, doc_t, tm_row, sc, dp, cm, cl, cd, st, st_in, acc, dq_t,
    sq, rq, sd, rd, sx, rx, sz, rz, fin, gq,
    o_s, i_s, z_s, z_r, y_s, y_r, x_s, x_r, c_s, c_r, st_s, st_r, q_s, q_r,
    d_s, d_r, xx_s, xx_r, zz_s, zz_r, h_s, h_r,
):
    ctx, head = lax.axis_index("ctx"), lax.axis_index("head")
    z, w = ctx // 4, ctx % 4
    x_lo, core = w // 2, w % 2
    x_hi, y = head // 4, head % 4
    x = 2 * x_hi + x_lo

    def device(zt, xt, yt, ct):
        return (zt * 4 + (xt % 2) * 2 + ct, (xt // 2) * 4 + yt)

    z_dev = lambda k: device((z + k) % 8, x, y, core)
    x_dev = lambda k: device(z, (x + k) % 4, y, core)
    y_dev = lambda k: device(z, x, (y + k) % 4, core)
    c_dev = device(z, x, y, 1 - core)
    h_dev = lambda k: (ctx, (head + k) % 8)

    def remote(src, dst, s, r, to):
        return pltpu.make_async_remote_copy(
            src_ref=src, dst_ref=dst, send_sem=s, recv_sem=r, device_id=to, device_id_type=MESH
        )

    barrier = pltpu.get_barrier_semaphore()
    peers = [z_dev(k) for k in range(1, 8)] + [x_dev(k) for k in range(1, 4)] + [c_dev]
    peers += [h_dev(k) for k in range(1, 8)]
    for peer in peers:
        pl.semaphore_signal(barrier, inc=1, device_id=peer, device_id_type=MESH)

    own_rows = pl.multiple_of(y * 32 + x_hi * 16, 16)

    def rows_of(xs, cs):
        return pl.ds(pl.multiple_of(((xs % 2) * 2 + cs) * 32 + (xs // 2) * 16, 16), 16)

    my_rows = rows_of(x, core)
    loads = []
    for high in (0, 1):
        theirs = pl.ds(own_rows + 128 * high, 16)
        loads.append((v_ref.at[theirs, :], kv.at[z, high, my_rows, pl.ds(0, 128)]))
        loads.append((k_ref.at[theirs, :], kv.at[z, high, my_rows, pl.ds(128, 128)]))
    for high in (0, 1):
        theirs = pl.ds(128 * high, 128)
        loads.append((do_ref.at[theirs, :], qd.at[high, y, :, pl.ds(0, 128)]))
        loads.append((q_ref.at[theirs, :], qd.at[high, y, :, pl.ds(128, 128)]))
    loads += [(doc_ref, doc_in), (tm_ref, tm_in)]
    loads = [pltpu.make_async_copy(a, b, i_s.at[n]) for n, (a, b) in enumerate(loads)]
    for load in loads:
        load.start()

    def clear(n, carry):
        acc[n, 0] = jnp.zeros((128, 256), F32)
        acc[n, 1] = jnp.zeros((128, 256), F32)
        return carry

    lax.fori_loop(0, 8, clear, 0)
    rz[...] = jnp.zeros((2, 8, 16, 256), BF)
    for load in loads[8:]:
        load.wait()

    doc_t[...] = jnp.concatenate([doc_in[...].astype(F32), jnp.zeros((64, 128), F32)], axis=0).T
    low_tile, high_tile = ctx, 63 - ctx
    lane32 = lax.broadcasted_iota(jnp.int32, (32, 128), 1)
    sub32 = lax.broadcasted_iota(jnp.int32, (32, 128), 0)
    doc_lane = (lane32 >= DOC_AT) & (lane32 < DOC_AT + 8)
    doc_of_lane = (lane32 - DOC_AT).astype(F32)

    docs_mine = doc_t[pl.ds(pl.multiple_of(y * 32, 32), 32), :]

    def key_features(t, carry):
        doc = jnp.sum(jnp.where(lane32 == t, docs_mine, 0.0), axis=1, keepdims=True)
        hit = (lane32 == t % TILES_MOD) | (doc_lane & (doc != doc_of_lane))
        low_lane = sub32 + jnp.where(t == low_tile, LOW_AT, 1000)
        high_lane = sub32 + jnp.where(t == high_tile, HIGH_AT, 1000)
        hit = hit | (lane32 == low_lane) | (lane32 == high_lane)
        high = t // 32
        at = jnp.where(high == 1, 63 - t, t)
        rows = pl.ds(pl.multiple_of((at % 4) * 32, 32), 32)
        kf[at // 4, high, rows, :] = jnp.where(hit, 1.0, 0.0).astype(BF)
        return carry

    lax.fori_loop(0, 64, key_features, 0, unroll=8)

    def query_features():
        lane = lax.broadcasted_iota(jnp.int32, (128, 128), 1)
        sub = lax.broadcasted_iota(jnp.int32, (128, 128), 0)
        for high in (0, 1):
            tile = high_tile if high else low_tile
            first = 28 - 4 * z if high else 0
            causal_at = HIGH_AT if high else LOW_AT
            doc = jnp.sum(jnp.where(lane == tile, doc_t[...], 0.0), axis=1, keepdims=True)
            tm_row[...] = jnp.zeros((8, 128), F32)
            tm_row[:, 0:64] = jnp.broadcast_to(tm_in[pl.ds(tile, 1), :].astype(F32), (8, 64))
            row = tm_row[...]
            row_far = pltpu.roll(row, 128 - TILES_MOD, 1)
            lane8 = lax.broadcasted_iota(jnp.int32, (8, 128), 1)
            near = lane8 >= first
            tile_at = jnp.where(near, lane8, lane8 + TILES_MOD)
            is_open = (jnp.where(near, row, row_far) > 0.5) & (tile_at <= tile)
            closed = jnp.where((lane8 < TILES_MOD) & jnp.logical_not(is_open), 1.0, 0.0)[0:1, :]
            hit = jnp.broadcast_to(closed, (128, 128)) > 0.5
            own_doc = doc == (lane - DOC_AT).astype(F32)
            hit = hit | ((lane >= DOC_AT) & (lane < DOC_AT + 8) & own_doc)
            later = (lane >= causal_at) & (lane < causal_at + 32) & (y * 32 + lane - causal_at > sub)
            qf[high] = jnp.where(hit | later, CLOSED, 0.0).astype(BF)

    query_features()
    for load in loads[:8]:
        load.wait()
    pl.semaphore_wait(barrier, len(peers))

    def piece(k, j, cs):
        return kv.at[(z + k) % 8, :, rows_of((x + 4 - j) % 4, cs), :]

    def z_copy(k):
        mine = piece(0, 0, core)
        return remote(mine, mine, z_s.at[k], z_r.at[k], z_dev(k))

    def x_copy(j, k):
        mine = piece(k, 0, core)
        return remote(mine, mine, x_s.at[j, k], x_r.at[j, k], x_dev(j))

    def c_copy(j, cs):
        theirs = kv.at[:, :, rows_of((x + 4 - j) % 4, cs), :]
        return remote(theirs, theirs, c_s.at[j], c_r.at[j], c_dev)

    for k in (4, 3, 5, 2, 6, 1, 7):
        z_copy(k).start()
    y_copies = []
    for k in (2, 1, 3):
        mine = qd.at[:, y]
        copy = remote(mine, mine, y_s.at[k], y_r.at[k], y_dev(k))
        copy.start()
        y_copies.append(copy)

    for k in (0, 1, 7, 2, 6, 3, 5, 4):
        if k:
            theirs = piece(8 - k, 0, core)
            remote(theirs, theirs, z_s.at[k], z_r.at[k], z_dev(k)).wait_recv()
        for j in (2, 1, 3):
            x_copy(j, (8 - k) % 8).start()
    c_copy(0, core).start()
    for j in (1, 3, 2):
        for k in (0, 7, 1, 6, 2, 5, 3, 4):
            theirs = piece(k, j, core)
            remote(theirs, theirs, x_s.at[j, k], x_r.at[j, k], x_dev(j)).wait_recv()
        c_copy(j, core).start()

    def send_waits():
        for k in range(8):
            if k:
                z_copy(k).wait_send()
            for j in (1, 2, 3):
                x_copy(j, k).wait_send()
        for j in range(4):
            c_copy(j, core).wait_send()

    for copy in y_copies:
        copy.wait()
    for j in range(4):
        c_copy(j, 1 - core).wait_recv()

    def query_rows(high):
        return jnp.concatenate([qd[high, a, :, 128:256] for a in range(4)], axis=0)

    def out_rows(high):
        return jnp.concatenate([qd[high, a, :, 0:128] for a in range(4)], axis=0)

    def low_chunk(i):
        return i, 0, 16 + i

    def high_chunk(i):
        near = i <= z
        plane = jnp.where(near, 7 - z + i, i - 1)
        return plane, jnp.where(near, 0, 1), jnp.where(near, plane, 8 + plane)

    chunk_of = (low_chunk, high_chunk)
    counts, groups = ((z + 2) // 2, 3), (2, 3)

    for high in (1, 0):

        group = groups[high]

        def scores(i, largest):
            chunks = [chunk_of[high](i * group + g) for g in range(group)]
            queries = jnp.concatenate(
                [query_rows(high), jnp.concatenate([qf[high]] * 4, axis=0)], axis=1
            )
            keys = [
                jnp.concatenate([kv[n, part, :, 128:256], kf[n, part]], axis=1)
                for n, part, slot in chunks
            ]
            values = [kv[n, part, :, 0:128] for n, part, slot in chunks]
            s = dot_nt(jnp.concatenate(keys, axis=0), queries)
            d = dot_nt(jnp.concatenate(values, axis=0), out_rows(high))
            largest = list(largest)
            for g, (n, part, slot) in enumerate(chunks):
                rows = slice(128 * g, 128 * g + 128)
                dp[slot] = d[rows]
                for a in range(4):
                    cols = slice(128 * a, 128 * a + 128)
                    scaled = (s[rows, cols] * SCALE_2).reshape(16, 8, 128)
                    most = jnp.max(scaled, axis=0)
                    e = jnp.exp2(scaled - most[None])
                    sc[slot, :, cols] = e.reshape(128, 128)
                    cm[slot, a] = most
                    cl[slot, a] = jnp.sum(e, axis=0)
                    cd[slot, a] = jnp.sum(e * d[rows, cols].reshape(16, 8, 128), axis=0)
                    largest[a] = jnp.maximum(largest[a], most)
            return tuple(largest)

        start = (jnp.full((8, 128), -3e38, F32),) * 4
        largest = lax.fori_loop(0, counts[high], scores, start)
        largest = [jnp.max(m, axis=0, keepdims=True) for m in largest]

        def sums(i, carry):
            totals, deltas = list(carry[0:4]), list(carry[4:8])
            for g in range(group):
                slot = chunk_of[high](i * group + g)[2]
                for a in range(4):
                    weight = jnp.exp2(cm[slot, a] - largest[a])
                    totals[a] += weight * cl[slot, a]
                    deltas[a] += weight * cd[slot, a]
            return tuple(totals + deltas)

        carry = lax.fori_loop(0, counts[high], sums, (jnp.zeros((8, 128), F32),) * 8)
        for a in range(4):
            st[high, a : a + 1, :] = largest[a]
            st[high, 4 + a : 5 + a, :] = jnp.sum(carry[a], axis=0, keepdims=True)
            st[high, 8 + a : 9 + a, :] = jnp.sum(carry[4 + a], axis=0, keepdims=True)
        st[high, 12:16, :] = jnp.zeros((4, 128), F32)
        for k in (2, 1, 3):
            remote(
                st.at[high], st_in.at[k, high], st_s.at[high, k], st_r.at[high, k], y_dev(k)
            ).start()

    def row_stats(high):
        for k in (1, 3, 2):
            remote(
                st.at[high], st_in.at[k, high], st_s.at[high, k], st_r.at[high, k], y_dev(k)
            ).wait()
        parts = [st[high]] + [st_in[k, high] for k in (1, 2, 3)]
        most = functools.reduce(jnp.maximum, [p[0:4, :] for p in parts])
        weights = [jnp.exp2(p[0:4, :] - most) for p in parts]
        total = sum(wt * p[4:8, :] for wt, p in zip(weights, parts))
        delta = sum(wt * p[8:12, :] for wt, p in zip(weights, parts)) / total
        return most, 1.0 / total, delta

    def grads_of(high, most, share, delta):
        def grads(i, carry):
            n, part, slot = chunk_of[high](i)
            probs, grad_s = [], []
            for a in range(4):
                cols = slice(128 * a, 128 * a + 128)
                factor = jnp.exp2(cm[slot, a] - most[a : a + 1, :]) * share[a : a + 1, :]
                p = (sc[slot, :, cols].reshape(16, 8, 128) * factor[None]).reshape(128, 128)
                probs.append(p.astype(BF))
                grad_s.append((p * (dp[slot, :, cols] - delta[a : a + 1, :])).astype(BF))
            probs, grad_s = jnp.concatenate(probs, axis=1), jnp.concatenate(grad_s, axis=1)
            acc[n, part, :, 0:128] += dot_nn(probs, out_rows(high))
            acc[n, part, :, 128:256] += dot_nn(grad_s, query_rows(high))
            dq_t[high] += dot_tn(kv[n, part, :, 128:256], grad_s)
            return carry

        return grads

    def d_copy(part, half):
        return remote(
            sd.at[part, half], rd.at[part, half], d_s.at[part, half], d_r.at[part, half], c_dev
        )

    def split(part, half):
        def step(n, carry):
            for h in (0, 1):
                rows = pl.ds(pl.multiple_of((2 * h + 1 - core) * 32, 32), 32)
                sd[part, half, n, h] = acc[4 * half + n, part, rows, :].astype(BF)
            return carry

        lax.fori_loop(0, 4, step, 0, unroll=True)
        d_copy(part, half).start()

    def xx_copy(part, half, k):
        return remote(
            sx.at[part, half, (x + k) % 4], rx.at[part, half, k],
            xx_s.at[part, half, k], xx_r.at[part, half, k], x_dev(k),
        )

    def sum_cores(part, half):
        d_copy(part, half).wait()

        def step(n, carry):
            for h in (0, 1):
                rows = pl.ds(pl.multiple_of((2 * h + core) * 32, 32), 32)
                both = acc[4 * half + n, part, rows, :] + rd[part, half, n, h].astype(F32)
                both = both.astype(BF)
                sx[part, half, h, n] = both[0:16]
                sx[part, half, 2 + h, n] = both[16:32]
            return carry

        lax.fori_loop(0, 4, step, 0, unroll=True)
        for k in (2, 1, 3):
            xx_copy(part, half, k).start()

    def zz_copy(part, k):
        return remote(
            sz.at[part, (z + k) % 8], rz.at[part, k], zz_s.at[part, k], zz_r.at[part, k], z_dev(k)
        )

    def meets(part, source, target):
        return (target >= source) if part else ((target <= source) | (target >= 7 - source))

    def sum_x(part, half):
        for k in (1, 3, 2):
            xx_copy(part, half, k).wait()

        def step(n, carry):
            total = sx[part, half, x, n].astype(F32)
            total += sum(rx[part, half, k, n].astype(F32) for k in (1, 2, 3))
            sz[part, 4 * half + n] = total.astype(BF)
            return carry

        lax.fori_loop(0, 4, step, 0, unroll=True)
        for k in (4, 3, 5, 2, 6, 1, 7):
            target = (z + k) % 8

            @pl.when((target // 4 == half) & meets(part, z, target))
            def _():
                zz_copy(part, k).start()

    def h_copy(part, k):
        mine = fin.at[part, pl.ds(own_rows, 16), :]
        return remote(mine, mine, h_s.at[part, k], h_r.at[part, k], h_dev(k))

    def sum_z(part):
        for k in (1, 7, 2, 6, 3, 5, 4):

            @pl.when(meets(part, (z + 8 - k) % 8, z))
            def _():
                zz_copy(part, k).wait_recv()

        total = sz[part, z].astype(F32) + sum(rz[part, k].astype(F32) for k in range(1, 8))
        total = jnp.concatenate([total[:, 0:128], total[:, 128:256] * SCALE], axis=1)
        fin[part, pl.ds(own_rows, 16), :] = total.astype(BF)
        for k in (6, 2, 4, 1, 3, 5, 7):
            h_copy(part, k).start()

    def stores(part):
        rows = pl.ds(128 * part, 128)
        return [
            pltpu.make_async_copy(fin.at[part, :, pl.ds(0, 128)], gv_ref.at[rows, :], o_s.at[part, 0]),
            pltpu.make_async_copy(fin.at[part, :, pl.ds(128, 128)], gk_ref.at[rows, :], o_s.at[part, 1]),
        ]

    def gathered(part):
        for k in (4, 1, 7, 3, 5, 2, 6):
            sender = (head + 8 - k) % 8
            rows = pl.multiple_of((sender % 4) * 32 + (sender // 4) * 16, 16)
            theirs = fin.at[part, pl.ds(rows, 16), :]
            remote(theirs, theirs, h_s.at[part, k], h_r.at[part, k], h_dev(k)).wait_recv()
        for copy in stores(part):
            copy.start()

    dq_t[...] = jnp.zeros((2, 128, 512), F32)
    high_grads = grads_of(1, *row_stats(1))
    lax.fori_loop(jnp.maximum(z, 4) + 1, 9, high_grads, 0)
    split(1, 1)

    @pl.when(z < 4)
    def _():
        lax.fori_loop(z + 1, 5, high_grads, 0)
        split(1, 0)

    low_grads = grads_of(0, *row_stats(0))
    sum_cores(1, 1)
    lax.fori_loop(0, jnp.minimum(z + 1, 4), low_grads, 0)
    lax.fori_loop(0, jnp.maximum(z - 3, 0), high_grads, 0)
    split(0, 0)

    @pl.when(z < 4)
    def _():
        sum_cores(1, 0)

    lax.fori_loop(4, jnp.maximum(z + 1, 4), low_grads, 0)
    lax.fori_loop(jnp.maximum(z - 3, 0), z + 1, high_grads, 0)
    split(0, 1)

    sum_cores(0, 0)
    for a in range(4):
        for high in (0, 1):
            rows = slice(128 * high, 128 * high + 128)
            sq[a, rows, :] = dq_t[high, :, 128 * a : 128 * a + 128].T.astype(BF)
    sum_cores(0, 1)
    q_copies = []
    for k in (2, 1, 3):
        copy = remote(sq.at[(y + k) % 4], rq.at[k], q_s.at[k], q_r.at[k], y_dev(k))
        copy.start()
        q_copies.append(copy)
    sum_x(1, 1)

    @pl.when(z < 4)
    def _():
        sum_x(1, 0)

    sum_x(0, 0)
    send_waits()
    sum_x(0, 1)
    for copy in q_copies:
        copy.wait()
    total = sq[y].astype(F32) + sum(rq[k].astype(F32) for k in (1, 2, 3))
    gq[...] = (SCALE * total).astype(BF)
    gq_store = pltpu.make_async_copy(gq, gq_ref, o_s.at[2, 0])
    gq_store.start()
    sum_z(1)
    sum_z(0)
    gathered(1)
    gathered(0)
    for part in (1, 0):
        for k in range(1, 8):
            h_copy(part, k).wait_send()

            @pl.when(meets(part, z, (z + k) % 8))
            def _():
                zz_copy(part, k).wait_send()

        for copy in stores(part):
            copy.wait()
    gq_store.wait()


def write_out(a, b, c, a_out, b_out, c_out, a_mid, b_mid, c_mid, sems):
    mids = (a_mid, b_mid, c_mid)
    first = [pltpu.make_async_copy(r, m, sems.at[n, 0]) for n, (r, m) in enumerate(zip((a, b, c), mids))]
    last = [pltpu.make_async_copy(m, r, sems.at[n, 1]) for n, (r, m) in enumerate(zip((a_out, b_out, c_out), mids))]
    for copy in first:
        copy.start()
    for one, two in zip(first, last):
        one.wait()
        two.start()
    for copy in last:
        copy.wait()


def body(query, key, value, grad_out, doc_ids, tile_mask):
    hbm = pl.BlockSpec(memory_space=pltpu.HBM)
    dma = lambda *shape: pltpu.SemaphoreType.DMA(shape)
    scratch = [
        pltpu.VMEM((8, 2, 128, 256), BF),
        pltpu.VMEM((8, 2, 128, 128), BF),
        pltpu.VMEM((2, 4, 128, 256), BF),
        pltpu.VMEM((2, 128, 128), BF),
        pltpu.VMEM((64, 128), jnp.int32),
        pltpu.VMEM((64, 64), jnp.int32),
        pltpu.VMEM((128, 128), F32),
        pltpu.VMEM((8, 128), F32),
        pltpu.VMEM((24, 128, 512), F32),
        pltpu.VMEM((24, 128, 512), F32),
        pltpu.VMEM((24, 4, 8, 128), F32),
        pltpu.VMEM((24, 4, 8, 128), F32),
        pltpu.VMEM((24, 4, 8, 128), F32),
        pltpu.VMEM((2, 16, 128), F32),
        pltpu.VMEM((4, 2, 16, 128), F32),
        pltpu.VMEM((8, 2, 128, 256), F32),
        pltpu.VMEM((2, 128, 512), F32),
        pltpu.VMEM((4, 256, 128), BF),
        pltpu.VMEM((4, 256, 128), BF),
        pltpu.VMEM((2, 2, 4, 2, 32, 256), BF),
        pltpu.VMEM((2, 2, 4, 2, 32, 256), BF),
        pltpu.VMEM((2, 2, 4, 4, 16, 256), BF),
        pltpu.VMEM((2, 2, 4, 4, 16, 256), BF),
        pltpu.VMEM((2, 8, 16, 256), BF),
        pltpu.VMEM((2, 8, 16, 256), BF),
        pltpu.VMEM((2, 128, 256), BF),
        pltpu.VMEM((256, 128), BF),
        dma(3, 2),
        dma(10), dma(8), dma(8), dma(4), dma(4), dma(4, 8), dma(4, 8), dma(4), dma(4),
        dma(2, 4), dma(2, 4), dma(4), dma(4),
        dma(2, 2), dma(2, 2), dma(2, 2, 4), dma(2, 2, 4), dma(2, 8), dma(2, 8), dma(2, 8), dma(2, 8),
    ]
    grad_query, grad_key, grad_value = pl.pallas_call(
        kernel,
        out_shape=[jax.ShapeDtypeStruct((256, 128), BF)] * 3,
        in_specs=[hbm] * 6,
        out_specs=[hbm] * 3,
        scratch_shapes=scratch,
        compiler_params=pltpu.CompilerParams(
            collective_id=0, has_side_effects=True, vmem_limit_bytes=56 << 20
        ),
        cost_estimate=pl.CostEstimate(flops=3 << 30, bytes_accessed=1 << 20, transcendentals=1 << 20),
        name="attention_grads",
    )(
        query.reshape(256, 128),
        grad_out.reshape(256, 128),
        key,
        value,
        doc_ids.reshape(64, 128),
        tile_mask,
    )
    grad_query, grad_key, grad_value = pl.pallas_call(
        write_out,
        out_shape=[jax.ShapeDtypeStruct((256, 128), BF)] * 3,
        in_specs=[hbm] * 3,
        out_specs=[hbm] * 3,
        scratch_shapes=[pltpu.VMEM((256, 128), BF)] * 3 + [dma(3, 2)],
        compiler_params=pltpu.CompilerParams(vmem_limit_bytes=56 << 20),
        name="write_out",
    )(grad_query, grad_key, grad_value)
    return grad_query.reshape(256, 1, 128), grad_key, grad_value


def solution(mesh):
    rows, heads = P("ctx", None), P("ctx", "head", None)
    return jax.shard_map(
        body,
        mesh=mesh,
        in_specs=(heads, rows, rows, heads, P(), P()),
        out_specs=(heads, rows, rows),
        check_vma=False,
    )
```

```python
import functools

import jax
import jax.numpy as jnp
from jax import lax
from jax.experimental import pallas as pl
from jax.experimental.pallas import tpu as pltpu
from jax.sharding import PartitionSpec as P

MESH = pl.DeviceIdType.MESH
BF, F32 = jnp.bfloat16, jnp.float32
SCALE = 128 ** -0.5
SCALE_2 = SCALE * 1.4426950408889634
CLOSED = -131072.0
TILES_MOD, DOC_AT, LOW_AT, HIGH_AT = 48, 48, 56, 88


def dot_nt(a, b):
    return lax.dot_general(a, b, (((1,), (1,)), ((), ())), preferred_element_type=F32)


def dot_nn(a, b):
    return lax.dot_general(a, b, (((1,), (0,)), ((), ())), preferred_element_type=F32)


def dot_tn(a, b):
    return lax.dot_general(a, b, (((0,), (0,)), ((), ())), preferred_element_type=F32)


def kernel(
    q_ref, do_ref, k_ref, v_ref, doc_ref, tm_ref,
    gq_ref, gk_ref, gv_ref,
    kv, kf, qd, qf, doc_in, tm_in, doc_t, tm_row, sc, dp, cm, cl, cd, st, st_in, acc, dq_t,
    sq, rq, sd, rd, sx, rx, sz, rz, fin, gq,
    o_s, i_s, z_s, z_r, y_s, y_r, x_s, x_r, c_s, c_r, st_s, st_r, q_s, q_r,
    d_s, d_r, xx_s, xx_r, zz_s, zz_r, h_s, h_r,
):
    ctx, head = lax.axis_index("ctx"), lax.axis_index("head")
    z, w = ctx // 4, ctx % 4
    x_lo, core = w // 2, w % 2
    x_hi, y = head // 4, head % 4
    x = 2 * x_hi + x_lo

    def device(zt, xt, yt, ct):
        return (zt * 4 + (xt % 2) * 2 + ct, (xt // 2) * 4 + yt)

    z_dev = lambda k: device((z + k) % 8, x, y, core)
    x_dev = lambda k: device(z, (x + k) % 4, y, core)
    y_dev = lambda k: device(z, x, (y + k) % 4, core)
    c_dev = device(z, x, y, 1 - core)
    h_dev = lambda k: (ctx, (head + k) % 8)

    def remote(src, dst, s, r, to):
        return pltpu.make_async_remote_copy(
            src_ref=src, dst_ref=dst, send_sem=s, recv_sem=r, device_id=to, device_id_type=MESH
        )

    barrier = pltpu.get_barrier_semaphore()
    peers = [z_dev(k) for k in range(1, 8)] + [x_dev(k) for k in range(1, 4)] + [c_dev]
    peers += [h_dev(k) for k in range(1, 8)]
    for peer in peers:
        pl.semaphore_signal(barrier, inc=1, device_id=peer, device_id_type=MESH)

    own_rows = pl.multiple_of(y * 32 + x_hi * 16, 16)

    def rows_of(xs, cs):
        return pl.ds(pl.multiple_of(((xs % 2) * 2 + cs) * 32 + (xs // 2) * 16, 16), 16)

    my_rows = rows_of(x, core)
    loads = []
    for high in (0, 1):
        theirs = pl.ds(own_rows + 128 * high, 16)
        loads.append((v_ref.at[theirs, :], kv.at[z, high, my_rows, pl.ds(0, 128)]))
        loads.append((k_ref.at[theirs, :], kv.at[z, high, my_rows, pl.ds(128, 128)]))
    for high in (0, 1):
        theirs = pl.ds(128 * high, 128)
        loads.append((do_ref.at[theirs, :], qd.at[high, y, :, pl.ds(0, 128)]))
        loads.append((q_ref.at[theirs, :], qd.at[high, y, :, pl.ds(128, 128)]))
    loads += [(doc_ref, doc_in), (tm_ref, tm_in)]
    loads = [pltpu.make_async_copy(a, b, i_s.at[n]) for n, (a, b) in enumerate(loads)]
    for load in loads:
        load.start()

    rz[...] = jnp.zeros((2, 8, 16, 256), BF)
    for load in loads[:4]:
        load.wait()
    pl.semaphore_wait(barrier, len(peers))

    def piece(k, j, cs):
        return kv.at[(z + k) % 8, :, rows_of((x + 4 - j) % 4, cs), :]

    def wanted(part, plane, reader):
        if part:
            return plane >= reader
        return (plane <= jnp.maximum(reader, 3)) | (plane >= 7 - reader)

    def z_copy(k, part):
        mine = piece(0, 0, core).at[part]
        return remote(mine, mine, z_s.at[k, part], z_r.at[k, part], z_dev(k))

    def z_take(k, part):
        theirs = piece(8 - k, 0, core).at[part]
        return remote(theirs, theirs, z_s.at[k, part], z_r.at[k, part], z_dev(k))

    def x_copy(j, k, part):
        mine = piece(k, 0, core).at[part]
        return remote(mine, mine, x_s.at[j, k, part], x_r.at[j, k, part], x_dev(j))

    def x_take(j, k, part):
        theirs = piece(k, j, core).at[part]
        return remote(theirs, theirs, x_s.at[j, k, part], x_r.at[j, k, part], x_dev(j))

    def c_copy(j, cs):
        theirs = kv.at[:, :, rows_of((x + 4 - j) % 4, cs), :]
        return remote(theirs, theirs, c_s.at[j], c_r.at[j], c_dev)

    for k in (4, 3, 5, 2, 6, 1, 7):
        for part in (0, 1):

            @pl.when(wanted(part, z, (z + k) % 8))
            def _():
                z_copy(k, part).start()

    for load in loads[4:8]:
        load.wait()
    y_copies = []
    for k in (2, 1, 3):
        mine = qd.at[:, y]
        copy = remote(mine, mine, y_s.at[k], y_r.at[k], y_dev(k))
        copy.start()
        y_copies.append(copy)

    for j in (2, 1, 3):
        for part in (0, 1):
            x_copy(j, 0, part).start()

    def clear(n, carry):
        acc[n, 0] = jnp.zeros((128, 256), F32)
        acc[n, 1] = jnp.zeros((128, 256), F32)
        return carry

    lax.fori_loop(0, 8, clear, 0)
    for load in loads[8:]:
        load.wait()

    doc_t[...] = jnp.concatenate([doc_in[...].astype(F32), jnp.zeros((64, 128), F32)], axis=0).T
    low_tile, high_tile = ctx, 63 - ctx
    lane32 = lax.broadcasted_iota(jnp.int32, (32, 128), 1)
    sub32 = lax.broadcasted_iota(jnp.int32, (32, 128), 0)
    doc_lane = (lane32 >= DOC_AT) & (lane32 < DOC_AT + 8)
    doc_of_lane = (lane32 - DOC_AT).astype(F32)

    docs_mine = doc_t[pl.ds(pl.multiple_of(y * 32, 32), 32), :]

    def key_features(t, carry):
        doc = jnp.sum(jnp.where(lane32 == t, docs_mine, 0.0), axis=1, keepdims=True)
        hit = (lane32 == t % TILES_MOD) | (doc_lane & (doc != doc_of_lane))
        low_lane = sub32 + jnp.where(t == low_tile, LOW_AT, 1000)
        high_lane = sub32 + jnp.where(t == high_tile, HIGH_AT, 1000)
        hit = hit | (lane32 == low_lane) | (lane32 == high_lane)
        high = t // 32
        at = jnp.where(high == 1, 63 - t, t)
        rows = pl.ds(pl.multiple_of((at % 4) * 32, 32), 32)
        kf[at // 4, high, rows, :] = jnp.where(hit, 1.0, 0.0).astype(BF)
        return carry

    lax.fori_loop(0, 64, key_features, 0, unroll=8)

    def query_features():
        lane = lax.broadcasted_iota(jnp.int32, (128, 128), 1)
        sub = lax.broadcasted_iota(jnp.int32, (128, 128), 0)
        for high in (0, 1):
            tile = high_tile if high else low_tile
            first = 28 - 4 * z if high else 0
            causal_at = HIGH_AT if high else LOW_AT
            doc = jnp.sum(jnp.where(lane == tile, doc_t[...], 0.0), axis=1, keepdims=True)
            tm_row[...] = jnp.zeros((8, 128), F32)
            tm_row[:, 0:64] = jnp.broadcast_to(tm_in[pl.ds(tile, 1), :].astype(F32), (8, 64))
            row = tm_row[...]
            row_far = pltpu.roll(row, 128 - TILES_MOD, 1)
            lane8 = lax.broadcasted_iota(jnp.int32, (8, 128), 1)
            near = lane8 >= first
            tile_at = jnp.where(near, lane8, lane8 + TILES_MOD)
            is_open = (jnp.where(near, row, row_far) > 0.5) & (tile_at <= tile)
            closed = jnp.where((lane8 < TILES_MOD) & jnp.logical_not(is_open), 1.0, 0.0)[0:1, :]
            hit = jnp.broadcast_to(closed, (128, 128)) > 0.5
            own_doc = doc == (lane - DOC_AT).astype(F32)
            hit = hit | ((lane >= DOC_AT) & (lane < DOC_AT + 8) & own_doc)
            later = (lane >= causal_at) & (lane < causal_at + 32) & (y * 32 + lane - causal_at > sub)
            qf[high] = jnp.where(hit | later, CLOSED, 0.0).astype(BF)

    query_features()

    for k in (1, 7, 2, 6, 3, 5, 4):
        for part in (0, 1):

            @pl.when(wanted(part, (z + 8 - k) % 8, z))
            def _():
                z_take(k, part).wait_recv()
                for j in (2, 1, 3):
                    x_copy(j, 8 - k, part).start()

    c_copy(0, core).start()
    for j in (1, 3, 2):
        for k in (0, 7, 1, 6, 2, 5, 3, 4):
            for part in (0, 1):

                @pl.when(wanted(part, (z + k) % 8, z))
                def _():
                    x_take(j, k, part).wait_recv()

        c_copy(j, core).start()

    def send_waits():
        for k in range(8):
            for part in (0, 1):
                if k:

                    @pl.when(wanted(part, z, (z + k) % 8))
                    def _():
                        z_copy(k, part).wait_send()

                @pl.when(wanted(part, (z + k) % 8, z))
                def _():
                    for j in (1, 2, 3):
                        x_copy(j, k, part).wait_send()

        for j in range(4):
            c_copy(j, core).wait_send()

    for copy in y_copies:
        copy.wait()
    for j in range(4):
        c_copy(j, 1 - core).wait_recv()

    def query_rows(high):
        return jnp.concatenate([qd[high, a, :, 128:256] for a in range(4)], axis=0)

    def out_rows(high):
        return jnp.concatenate([qd[high, a, :, 0:128] for a in range(4)], axis=0)

    def low_chunk(i):
        return i, 0, 16 + i

    def high_chunk(i):
        near = i <= z
        plane = jnp.where(near, 7 - z + i, i - 1)
        return plane, jnp.where(near, 0, 1), jnp.where(near, plane, 8 + plane)

    chunk_of = (low_chunk, high_chunk)
    counts, groups = ((z + 4) // 4, 3), (4, 3)

    for high in (1, 0):

        group = groups[high]

        def scores(i, largest):
            chunks = [chunk_of[high](i * group + g) for g in range(group)]
            queries = jnp.concatenate(
                [query_rows(high), jnp.concatenate([qf[high]] * 4, axis=0)], axis=1
            )
            keys = [
                jnp.concatenate([kv[n, part, :, 128:256], kf[n, part]], axis=1)
                for n, part, slot in chunks
            ]
            values = [kv[n, part, :, 0:128] for n, part, slot in chunks]
            s = dot_nt(jnp.concatenate(keys, axis=0), queries)
            d = dot_nt(jnp.concatenate(values, axis=0), out_rows(high))
            largest = list(largest)
            for g, (n, part, slot) in enumerate(chunks):
                rows = slice(128 * g, 128 * g + 128)
                dp[slot] = d[rows]
                for a in range(4):
                    cols = slice(128 * a, 128 * a + 128)
                    scaled = (s[rows, cols] * SCALE_2).reshape(16, 8, 128)
                    most = jnp.max(scaled, axis=0)
                    e = jnp.exp2(scaled - most[None])
                    sc[slot, :, cols] = e.reshape(128, 128)
                    cm[slot, a] = most
                    cl[slot, a] = jnp.sum(e, axis=0)
                    cd[slot, a] = jnp.sum(e * d[rows, cols].reshape(16, 8, 128), axis=0)
                    largest[a] = jnp.maximum(largest[a], most)
            return tuple(largest)

        start = (jnp.full((8, 128), -3e38, F32),) * 4
        largest = lax.fori_loop(0, counts[high], scores, start)
        largest = [jnp.max(m, axis=0, keepdims=True) for m in largest]

        def sums(i, carry):
            totals, deltas = list(carry[0:4]), list(carry[4:8])
            for g in range(group):
                slot = chunk_of[high](i * group + g)[2]
                for a in range(4):
                    weight = jnp.exp2(cm[slot, a] - largest[a])
                    totals[a] += weight * cl[slot, a]
                    deltas[a] += weight * cd[slot, a]
            return tuple(totals + deltas)

        carry = lax.fori_loop(0, counts[high], sums, (jnp.zeros((8, 128), F32),) * 8)
        for a in range(4):
            st[high, a : a + 1, :] = largest[a]
            st[high, 4 + a : 5 + a, :] = jnp.sum(carry[a], axis=0, keepdims=True)
            st[high, 8 + a : 9 + a, :] = jnp.sum(carry[4 + a], axis=0, keepdims=True)
        st[high, 12:16, :] = jnp.zeros((4, 128), F32)
        for k in (2, 1, 3):
            remote(
                st.at[high], st_in.at[k, high], st_s.at[high, k], st_r.at[high, k], y_dev(k)
            ).start()

    def row_stats(high):
        for k in (1, 3, 2):
            remote(
                st.at[high], st_in.at[k, high], st_s.at[high, k], st_r.at[high, k], y_dev(k)
            ).wait()
        parts = [st[high]] + [st_in[k, high] for k in (1, 2, 3)]
        most = functools.reduce(jnp.maximum, [p[0:4, :] for p in parts])
        weights = [jnp.exp2(p[0:4, :] - most) for p in parts]
        total = sum(wt * p[4:8, :] for wt, p in zip(weights, parts))
        delta = sum(wt * p[8:12, :] for wt, p in zip(weights, parts)) / total
        return most, 1.0 / total, delta

    def grads_of(high, most, share, delta):
        group = groups[high]

        def grads(i, carry):
            chunks = [chunk_of[high](i * group + g) for g in range(group)]
            probs, grad_s = [], []
            for n, part, slot in chunks:
                probs_row, grad_row = [], []
                for a in range(4):
                    cols = slice(128 * a, 128 * a + 128)
                    factor = jnp.exp2(cm[slot, a] - most[a : a + 1, :]) * share[a : a + 1, :]
                    p = (sc[slot, :, cols].reshape(16, 8, 128) * factor[None]).reshape(128, 128)
                    probs_row.append(p.astype(BF))
                    grad_row.append((p * (dp[slot, :, cols] - delta[a : a + 1, :])).astype(BF))
                probs.append(jnp.concatenate(probs_row, axis=1))
                grad_s.append(jnp.concatenate(grad_row, axis=1))
            probs, grad_s = jnp.concatenate(probs, axis=0), jnp.concatenate(grad_s, axis=0)
            value_part = dot_nn(probs, out_rows(high))
            key_part = dot_nn(grad_s, query_rows(high))
            for g, (n, part, slot) in enumerate(chunks):
                rows = slice(128 * g, 128 * g + 128)
                acc[n, part, :, 0:128] += value_part[rows]
                acc[n, part, :, 128:256] += key_part[rows]
            keys = jnp.concatenate([kv[n, part, :, 128:256] for n, part, slot in chunks], axis=0)
            dq_t[high] += dot_tn(keys, grad_s)
            return carry

        return grads

    def d_copy(part, half):
        return remote(
            sd.at[part, half], rd.at[part, half], d_s.at[part, half], d_r.at[part, half], c_dev
        )

    def split(part, half):
        def step(n, carry):
            for h in (0, 1):
                rows = pl.ds(pl.multiple_of((2 * h + 1 - core) * 32, 32), 32)
                sd[part, half, n, h] = acc[4 * half + n, part, rows, :].astype(BF)
            return carry

        lax.fori_loop(0, 4, step, 0, unroll=True)
        d_copy(part, half).start()

    def xx_copy(part, half, k):
        return remote(
            sx.at[part, half, (x + k) % 4], rx.at[part, half, k],
            xx_s.at[part, half, k], xx_r.at[part, half, k], x_dev(k),
        )

    def sum_cores(part, half):
        d_copy(part, half).wait()

        def step(n, carry):
            for h in (0, 1):
                rows = pl.ds(pl.multiple_of((2 * h + core) * 32, 32), 32)
                both = acc[4 * half + n, part, rows, :] + rd[part, half, n, h].astype(F32)
                both = both.astype(BF)
                sx[part, half, h, n] = both[0:16]
                sx[part, half, 2 + h, n] = both[16:32]
            return carry

        lax.fori_loop(0, 4, step, 0, unroll=True)
        for k in (2, 1, 3):
            xx_copy(part, half, k).start()

    def zz_copy(part, k):
        return remote(
            sz.at[part, (z + k) % 8], rz.at[part, k], zz_s.at[part, k], zz_r.at[part, k], z_dev(k)
        )

    def meets(part, source, target):
        return (target >= source) if part else ((target <= source) | (target >= 7 - source))

    def sum_x(part, half):
        for k in (1, 3, 2):
            xx_copy(part, half, k).wait()

        def step(n, carry):
            total = sx[part, half, x, n].astype(F32)
            total += sum(rx[part, half, k, n].astype(F32) for k in (1, 2, 3))
            sz[part, 4 * half + n] = total.astype(BF)
            return carry

        lax.fori_loop(0, 4, step, 0, unroll=True)
        for k in (4, 3, 5, 2, 6, 1, 7):
            target = (z + k) % 8

            @pl.when((target // 4 == half) & meets(part, z, target))
            def _():
                zz_copy(part, k).start()

    def h_copy(part, k):
        mine = fin.at[part, pl.ds(own_rows, 16), :]
        return remote(mine, mine, h_s.at[part, k], h_r.at[part, k], h_dev(k))

    def sum_z(part):
        for k in (1, 7, 2, 6, 3, 5, 4):

            @pl.when(meets(part, (z + 8 - k) % 8, z))
            def _():
                zz_copy(part, k).wait_recv()

        total = sz[part, z].astype(F32) + sum(rz[part, k].astype(F32) for k in range(1, 8))
        total = jnp.concatenate([total[:, 0:128], total[:, 128:256] * SCALE], axis=1)
        fin[part, pl.ds(own_rows, 16), :] = total.astype(BF)
        for k in (6, 2, 4, 1, 3, 5, 7):
            h_copy(part, k).start()

    def stores(part):
        rows = pl.ds(128 * part, 128)
        return [
            pltpu.make_async_copy(fin.at[part, :, pl.ds(0, 128)], gv_ref.at[rows, :], o_s.at[part, 0]),
            pltpu.make_async_copy(fin.at[part, :, pl.ds(128, 128)], gk_ref.at[rows, :], o_s.at[part, 1]),
        ]

    def gathered(part):
        for k in (4, 1, 7, 3, 5, 2, 6):
            sender = (head + 8 - k) % 8
            rows = pl.multiple_of((sender % 4) * 32 + (sender // 4) * 16, 16)
            theirs = fin.at[part, pl.ds(rows, 16), :]
            remote(theirs, theirs, h_s.at[part, k], h_r.at[part, k], h_dev(k)).wait_recv()
        for copy in stores(part):
            copy.start()

    dq_t[...] = jnp.zeros((2, 128, 512), F32)
    high_grads = grads_of(1, *row_stats(1))
    lax.fori_loop(0, 3, high_grads, 0)
    split(1, 1)

    @pl.when(z < 4)
    def _():
        split(1, 0)

    low_grads = grads_of(0, *row_stats(0))
    sum_cores(1, 1)
    low_grads(0, 0)
    split(0, 0)

    @pl.when(z < 4)
    def _():
        sum_cores(1, 0)

    @pl.when(z >= 4)
    def _():
        low_grads(1, 0)

    split(0, 1)

    sum_cores(0, 0)
    for a in range(4):
        for high in (0, 1):
            rows = slice(128 * high, 128 * high + 128)
            sq[a, rows, :] = dq_t[high, :, 128 * a : 128 * a + 128].T.astype(BF)
    sum_cores(0, 1)
    q_copies = []
    for k in (2, 1, 3):
        copy = remote(sq.at[(y + k) % 4], rq.at[k], q_s.at[k], q_r.at[k], y_dev(k))
        copy.start()
        q_copies.append(copy)
    sum_x(1, 1)

    @pl.when(z < 4)
    def _():
        sum_x(1, 0)

    sum_x(0, 0)
    send_waits()
    sum_x(0, 1)
    for copy in q_copies:
        copy.wait()
    total = sq[y].astype(F32) + sum(rq[k].astype(F32) for k in (1, 2, 3))
    gq[...] = (SCALE * total).astype(BF)
    gq_store = pltpu.make_async_copy(gq, gq_ref, o_s.at[2, 0])
    gq_store.start()
    sum_z(1)
    sum_z(0)
    gathered(1)
    gathered(0)
    for part in (1, 0):
        for k in range(1, 8):
            h_copy(part, k).wait_send()

            @pl.when(meets(part, z, (z + k) % 8))
            def _():
                zz_copy(part, k).wait_send()

        for copy in stores(part):
            copy.wait()
    gq_store.wait()


def write_out(a, b, c, a_out, b_out, c_out, a_mid, b_mid, c_mid, sems):
    mids = (a_mid, b_mid, c_mid)
    first = [pltpu.make_async_copy(r, m, sems.at[n, 0]) for n, (r, m) in enumerate(zip((a, b, c), mids))]
    last = [pltpu.make_async_copy(m, r, sems.at[n, 1]) for n, (r, m) in enumerate(zip((a_out, b_out, c_out), mids))]
    for copy in first:
        copy.start()
    for one, two in zip(first, last):
        one.wait()
        two.start()
    for copy in last:
        copy.wait()


def body(query, key, value, grad_out, doc_ids, tile_mask):
    hbm = pl.BlockSpec(memory_space=pltpu.HBM)
    dma = lambda *shape: pltpu.SemaphoreType.DMA(shape)
    scratch = [
        pltpu.VMEM((8, 2, 128, 256), BF),
        pltpu.VMEM((8, 2, 128, 128), BF),
        pltpu.VMEM((2, 4, 128, 256), BF),
        pltpu.VMEM((2, 128, 128), BF),
        pltpu.VMEM((64, 128), jnp.int32),
        pltpu.VMEM((64, 64), jnp.int32),
        pltpu.VMEM((128, 128), F32),
        pltpu.VMEM((8, 128), F32),
        pltpu.VMEM((24, 128, 512), F32),
        pltpu.VMEM((24, 128, 512), F32),
        pltpu.VMEM((24, 4, 8, 128), F32),
        pltpu.VMEM((24, 4, 8, 128), F32),
        pltpu.VMEM((24, 4, 8, 128), F32),
        pltpu.VMEM((2, 16, 128), F32),
        pltpu.VMEM((4, 2, 16, 128), F32),
        pltpu.VMEM((8, 2, 128, 256), F32),
        pltpu.VMEM((2, 128, 512), F32),
        pltpu.VMEM((4, 256, 128), BF),
        pltpu.VMEM((4, 256, 128), BF),
        pltpu.VMEM((2, 2, 4, 2, 32, 256), BF),
        pltpu.VMEM((2, 2, 4, 2, 32, 256), BF),
        pltpu.VMEM((2, 2, 4, 4, 16, 256), BF),
        pltpu.VMEM((2, 2, 4, 4, 16, 256), BF),
        pltpu.VMEM((2, 8, 16, 256), BF),
        pltpu.VMEM((2, 8, 16, 256), BF),
        pltpu.VMEM((2, 128, 256), BF),
        pltpu.VMEM((256, 128), BF),
        dma(3, 2),
        dma(10), dma(8, 2), dma(8, 2), dma(4), dma(4), dma(4, 8, 2), dma(4, 8, 2), dma(4), dma(4),
        dma(2, 4), dma(2, 4), dma(4), dma(4),
        dma(2, 2), dma(2, 2), dma(2, 2, 4), dma(2, 2, 4), dma(2, 8), dma(2, 8), dma(2, 8), dma(2, 8),
    ]
    grad_query, grad_key, grad_value = pl.pallas_call(
        kernel,
        out_shape=[jax.ShapeDtypeStruct((256, 128), BF)] * 3,
        in_specs=[hbm] * 6,
        out_specs=[hbm] * 3,
        scratch_shapes=scratch,
        compiler_params=pltpu.CompilerParams(
            collective_id=0, has_side_effects=True, vmem_limit_bytes=56 << 20
        ),
        cost_estimate=pl.CostEstimate(flops=3 << 30, bytes_accessed=1 << 20, transcendentals=1 << 20),
        name="attention_grads",
    )(
        query.reshape(256, 128),
        grad_out.reshape(256, 128),
        key,
        value,
        doc_ids.reshape(64, 128),
        tile_mask,
    )
    grad_query, grad_key, grad_value = pl.pallas_call(
        write_out,
        out_shape=[jax.ShapeDtypeStruct((256, 128), BF)] * 3,
        in_specs=[hbm] * 3,
        out_specs=[hbm] * 3,
        scratch_shapes=[pltpu.VMEM((256, 128), BF)] * 3 + [dma(3, 2)],
        compiler_params=pltpu.CompilerParams(vmem_limit_bytes=56 << 20),
        name="write_out",
    )(grad_query, grad_key, grad_value)
    return grad_query.reshape(256, 1, 128), grad_key, grad_value


def solution(mesh):
    rows, heads = P("ctx", None), P("ctx", "head", None)
    return jax.shard_map(
        body,
        mesh=mesh,
        in_specs=(heads, rows, rows, heads, P(), P()),
        out_specs=(heads, rows, rows),
        check_vma=False,
    )
```

```python
import functools

import jax
import jax.numpy as jnp
from jax import lax
from jax.experimental import pallas as pl
from jax.experimental.pallas import tpu as pltpu
from jax.sharding import PartitionSpec as P

MESH = pl.DeviceIdType.MESH
BF, F32 = jnp.bfloat16, jnp.float32
SCALE = 128 ** -0.5
SCALE_2 = SCALE * 1.4426950408889634
CLOSED = -131072.0
TILES_MOD, DOC_AT, LOW_AT, HIGH_AT = 48, 48, 56, 88


def dot_nt(a, b):
    return lax.dot_general(a, b, (((1,), (1,)), ((), ())), preferred_element_type=F32)


def dot_nn(a, b):
    return lax.dot_general(a, b, (((1,), (0,)), ((), ())), preferred_element_type=F32)


def dot_tn(a, b):
    return lax.dot_general(a, b, (((0,), (0,)), ((), ())), preferred_element_type=F32)


def kernel(
    q_ref, do_ref, k_ref, v_ref, doc_ref, tm_ref,
    gq_ref, gk_ref, gv_ref,
    kv, kf, qd, qf, doc_in, tm_in, doc_t, tm_row, sc, dp, cm, cl, cd, st, st_in, acc, dq_t,
    sq, rq, sd, rd, sx, rx, sz, rz, fin, gq,
    o_s, i_s, z_s, z_r, y_s, y_r, x_s, x_r, c_s, c_r, st_s, st_r, q_s, q_r,
    d_s, d_r, xx_s, xx_r, zz_s, zz_r, h_s, h_r,
):
    ctx, head = lax.axis_index("ctx"), lax.axis_index("head")
    z, w = ctx // 4, ctx % 4
    x_lo, core = w // 2, w % 2
    x_hi, y = head // 4, head % 4
    x = 2 * x_hi + x_lo

    def device(zt, xt, yt, ct):
        return (zt * 4 + (xt % 2) * 2 + ct, (xt // 2) * 4 + yt)

    z_dev = lambda k: device((z + k) % 8, x, y, core)
    x_dev = lambda k: device(z, (x + k) % 4, y, core)
    y_dev = lambda k: device(z, x, (y + k) % 4, core)
    c_dev = device(z, x, y, 1 - core)
    h_dev = lambda k: (ctx, (head + k) % 8)

    def remote(src, dst, s, r, to):
        return pltpu.make_async_remote_copy(
            src_ref=src, dst_ref=dst, send_sem=s, recv_sem=r, device_id=to, device_id_type=MESH
        )

    barrier = pltpu.get_barrier_semaphore()
    peers = [z_dev(k) for k in range(1, 8)] + [x_dev(k) for k in range(1, 4)] + [c_dev]
    peers += [h_dev(k) for k in range(1, 8)]
    for peer in peers:
        pl.semaphore_signal(barrier, inc=1, device_id=peer, device_id_type=MESH)

    own_rows = pl.multiple_of(y * 32 + x_hi * 16, 16)

    def rows_of(xs, cs):
        return pl.ds(pl.multiple_of(((xs % 2) * 2 + cs) * 32 + (xs // 2) * 16, 16), 16)

    my_rows = rows_of(x, core)
    loads = []
    for high in (0, 1):
        theirs = pl.ds(own_rows + 128 * high, 16)
        loads.append((v_ref.at[theirs, :], kv.at[z, high, my_rows, pl.ds(0, 128)]))
        loads.append((k_ref.at[theirs, :], kv.at[z, high, my_rows, pl.ds(128, 128)]))
    for high in (0, 1):
        theirs = pl.ds(128 * high, 128)
        loads.append((do_ref.at[theirs, :], qd.at[high, y, :, pl.ds(0, 128)]))
        loads.append((q_ref.at[theirs, :], qd.at[high, y, :, pl.ds(128, 128)]))
    loads += [(doc_ref, doc_in), (tm_ref, tm_in)]
    loads = [pltpu.make_async_copy(a, b, i_s.at[n]) for n, (a, b) in enumerate(loads)]
    for load in loads:
        load.start()

    rz[...] = jnp.zeros((2, 8, 16, 256), BF)
    for load in loads[:4]:
        load.wait()
    pl.semaphore_wait(barrier, len(peers))

    def piece(k, j, cs):
        return kv.at[(z + k) % 8, :, rows_of((x + 4 - j) % 4, cs), :]

    def wanted(part, plane, reader):
        if part:
            return plane >= reader
        return (plane <= jnp.maximum(reader, 3)) | (plane >= 7 - reader)

    def z_copy(k, part):
        mine = piece(0, 0, core).at[part]
        return remote(mine, mine, z_s.at[k, part], z_r.at[k, part], z_dev(k))

    def z_take(k, part):
        theirs = piece(8 - k, 0, core).at[part]
        return remote(theirs, theirs, z_s.at[k, part], z_r.at[k, part], z_dev(k))

    def x_copy(j, k, part):
        mine = piece(k, 0, core).at[part]
        return remote(mine, mine, x_s.at[j, k, part], x_r.at[j, k, part], x_dev(j))

    def x_take(j, k, part):
        theirs = piece(k, j, core).at[part]
        return remote(theirs, theirs, x_s.at[j, k, part], x_r.at[j, k, part], x_dev(j))

    def c_copy(j, cs):
        theirs = kv.at[:, :, rows_of((x + 4 - j) % 4, cs), :]
        return remote(theirs, theirs, c_s.at[j], c_r.at[j], c_dev)

    for k in (4, 3, 5, 2, 6, 1, 7):
        for part in (0, 1):

            @pl.when(wanted(part, z, (z + k) % 8))
            def _():
                z_copy(k, part).start()

    for load in loads[4:8]:
        load.wait()
    y_copies = []
    for k in (2, 1, 3):
        mine = qd.at[:, y]
        copy = remote(mine, mine, y_s.at[k], y_r.at[k], y_dev(k))
        copy.start()
        y_copies.append(copy)

    for j in (2, 1, 3):
        for part in (0, 1):
            x_copy(j, 0, part).start()

    def clear(n, carry):
        acc[n, 0] = jnp.zeros((128, 256), F32)
        acc[n, 1] = jnp.zeros((128, 256), F32)
        return carry

    lax.fori_loop(0, 8, clear, 0)
    for load in loads[8:]:
        load.wait()

    doc_t[...] = jnp.concatenate([doc_in[...].astype(F32), jnp.zeros((64, 128), F32)], axis=0).T
    low_tile, high_tile = ctx, 63 - ctx
    lane32 = lax.broadcasted_iota(jnp.int32, (32, 128), 1)
    sub32 = lax.broadcasted_iota(jnp.int32, (32, 128), 0)
    doc_lane = (lane32 >= DOC_AT) & (lane32 < DOC_AT + 8)
    doc_of_lane = (lane32 - DOC_AT).astype(F32)

    docs_mine = doc_t[pl.ds(pl.multiple_of(y * 32, 32), 32), :]

    def key_features(t, carry):
        doc = jnp.sum(jnp.where(lane32 == t, docs_mine, 0.0), axis=1, keepdims=True)
        hit = (lane32 == t % TILES_MOD) | (doc_lane & (doc != doc_of_lane))
        low_lane = sub32 + jnp.where(t == low_tile, LOW_AT, 1000)
        high_lane = sub32 + jnp.where(t == high_tile, HIGH_AT, 1000)
        hit = hit | (lane32 == low_lane) | (lane32 == high_lane)
        high = t // 32
        at = jnp.where(high == 1, 63 - t, t)
        rows = pl.ds(pl.multiple_of((at % 4) * 32, 32), 32)
        kf[at // 4, high, rows, :] = jnp.where(hit, 1.0, 0.0).astype(BF)
        return carry

    lax.fori_loop(0, 64, key_features, 0, unroll=8)

    def query_features():
        lane = lax.broadcasted_iota(jnp.int32, (128, 128), 1)
        sub = lax.broadcasted_iota(jnp.int32, (128, 128), 0)
        for high in (0, 1):
            tile = high_tile if high else low_tile
            first = 28 - 4 * z if high else 0
            causal_at = HIGH_AT if high else LOW_AT
            doc = jnp.sum(jnp.where(lane == tile, doc_t[...], 0.0), axis=1, keepdims=True)
            tm_row[...] = jnp.zeros((8, 128), F32)
            tm_row[:, 0:64] = jnp.broadcast_to(tm_in[pl.ds(tile, 1), :].astype(F32), (8, 64))
            row = tm_row[...]
            row_far = pltpu.roll(row, 128 - TILES_MOD, 1)
            lane8 = lax.broadcasted_iota(jnp.int32, (8, 128), 1)
            near = lane8 >= first
            tile_at = jnp.where(near, lane8, lane8 + TILES_MOD)
            is_open = (jnp.where(near, row, row_far) > 0.5) & (tile_at <= tile)
            closed = jnp.where((lane8 < TILES_MOD) & jnp.logical_not(is_open), 1.0, 0.0)[0:1, :]
            hit = jnp.broadcast_to(closed, (128, 128)) > 0.5
            own_doc = doc == (lane - DOC_AT).astype(F32)
            hit = hit | ((lane >= DOC_AT) & (lane < DOC_AT + 8) & own_doc)
            later = (lane >= causal_at) & (lane < causal_at + 32) & (y * 32 + lane - causal_at > sub)
            qf[high] = jnp.where(hit | later, CLOSED, 0.0).astype(BF)

    query_features()

    for k in (1, 7, 2, 6, 3, 5, 4):
        for part in (0, 1):

            @pl.when(wanted(part, (z + 8 - k) % 8, z))
            def _():
                z_take(k, part).wait_recv()
                for j in (2, 1, 3):
                    x_copy(j, 8 - k, part).start()

    c_copy(0, core).start()
    for j in (1, 3, 2):
        for k in (0, 7, 1, 6, 2, 5, 3, 4):
            for part in (0, 1):

                @pl.when(wanted(part, (z + k) % 8, z))
                def _():
                    x_take(j, k, part).wait_recv()

        c_copy(j, core).start()

    def send_waits():
        for k in range(8):
            for part in (0, 1):
                if k:

                    @pl.when(wanted(part, z, (z + k) % 8))
                    def _():
                        z_copy(k, part).wait_send()

                @pl.when(wanted(part, (z + k) % 8, z))
                def _():
                    for j in (1, 2, 3):
                        x_copy(j, k, part).wait_send()

        for j in range(4):
            c_copy(j, core).wait_send()

    for copy in y_copies:
        copy.wait()
    for j in range(4):
        c_copy(j, 1 - core).wait_recv()

    def query_rows(high):
        return jnp.concatenate([qd[high, a, :, 128:256] for a in range(4)], axis=0)

    def out_rows(high):
        return jnp.concatenate([qd[high, a, :, 0:128] for a in range(4)], axis=0)

    def low_chunk(i):
        return i, 0, 16 + i

    def high_chunk(i):
        near = i <= z
        plane = jnp.where(near, 7 - z + i, i - 1)
        return plane, jnp.where(near, 0, 1), jnp.where(near, plane, 8 + plane)

    chunk_of = (low_chunk, high_chunk)
    counts, groups = ((z + 4) // 4, 1), (4, 9)

    for high in (1, 0):

        group = groups[high]

        def scores(i, largest):
            chunks = [chunk_of[high](i * group + g) for g in range(group)]
            queries = jnp.concatenate(
                [query_rows(high), jnp.concatenate([qf[high]] * 4, axis=0)], axis=1
            )
            keys = [
                jnp.concatenate([kv[n, part, :, 128:256], kf[n, part]], axis=1)
                for n, part, slot in chunks
            ]
            values = [kv[n, part, :, 0:128] for n, part, slot in chunks]
            s = dot_nt(jnp.concatenate(keys, axis=0), queries)
            d = dot_nt(jnp.concatenate(values, axis=0), out_rows(high))
            largest = list(largest)
            for g, (n, part, slot) in enumerate(chunks):
                rows = slice(128 * g, 128 * g + 128)
                dp[slot] = d[rows]
                for a in range(4):
                    cols = slice(128 * a, 128 * a + 128)
                    scaled = (s[rows, cols] * SCALE_2).reshape(16, 8, 128)
                    most = jnp.max(scaled, axis=0)
                    e = jnp.exp2(scaled - most[None])
                    sc[slot, :, cols] = e.reshape(128, 128)
                    cm[slot, a] = most
                    cl[slot, a] = jnp.sum(e, axis=0)
                    cd[slot, a] = jnp.sum(e * d[rows, cols].reshape(16, 8, 128), axis=0)
                    largest[a] = jnp.maximum(largest[a], most)
            return tuple(largest)

        start = (jnp.full((8, 128), -3e38, F32),) * 4
        largest = lax.fori_loop(0, counts[high], scores, start)
        largest = [jnp.max(m, axis=0, keepdims=True) for m in largest]

        def sums(i, carry):
            totals, deltas = list(carry[0:4]), list(carry[4:8])
            for g in range(group):
                slot = chunk_of[high](i * group + g)[2]
                for a in range(4):
                    weight = jnp.exp2(cm[slot, a] - largest[a])
                    totals[a] += weight * cl[slot, a]
                    deltas[a] += weight * cd[slot, a]
            return tuple(totals + deltas)

        carry = lax.fori_loop(0, counts[high], sums, (jnp.zeros((8, 128), F32),) * 8)
        for a in range(4):
            st[high, a : a + 1, :] = largest[a]
            st[high, 4 + a : 5 + a, :] = jnp.sum(carry[a], axis=0, keepdims=True)
            st[high, 8 + a : 9 + a, :] = jnp.sum(carry[4 + a], axis=0, keepdims=True)
        st[high, 12:16, :] = jnp.zeros((4, 128), F32)
        for k in (2, 1, 3):
            remote(
                st.at[high], st_in.at[k, high], st_s.at[high, k], st_r.at[high, k], y_dev(k)
            ).start()

    def row_stats(high):
        for k in (1, 3, 2):
            remote(
                st.at[high], st_in.at[k, high], st_s.at[high, k], st_r.at[high, k], y_dev(k)
            ).wait()
        parts = [st[high]] + [st_in[k, high] for k in (1, 2, 3)]
        most = functools.reduce(jnp.maximum, [p[0:4, :] for p in parts])
        weights = [jnp.exp2(p[0:4, :] - most) for p in parts]
        total = sum(wt * p[4:8, :] for wt, p in zip(weights, parts))
        delta = sum(wt * p[8:12, :] for wt, p in zip(weights, parts)) / total
        return most, 1.0 / total, delta

    def grads_of(high, most, share, delta):
        group = groups[high]

        def grads(i, carry):
            chunks = [chunk_of[high](i * group + g) for g in range(group)]
            probs, grad_s = [], []
            for n, part, slot in chunks:
                probs_row, grad_row = [], []
                for a in range(4):
                    cols = slice(128 * a, 128 * a + 128)
                    factor = jnp.exp2(cm[slot, a] - most[a : a + 1, :]) * share[a : a + 1, :]
                    p = (sc[slot, :, cols].reshape(16, 8, 128) * factor[None]).reshape(128, 128)
                    probs_row.append(p.astype(BF))
                    grad_row.append((p * (dp[slot, :, cols] - delta[a : a + 1, :])).astype(BF))
                probs.append(jnp.concatenate(probs_row, axis=1))
                grad_s.append(jnp.concatenate(grad_row, axis=1))
            probs, grad_s = jnp.concatenate(probs, axis=0), jnp.concatenate(grad_s, axis=0)
            value_part = dot_nn(probs, out_rows(high))
            key_part = dot_nn(grad_s, query_rows(high))
            for g, (n, part, slot) in enumerate(chunks):
                rows = slice(128 * g, 128 * g + 128)
                acc[n, part, :, 0:128] += value_part[rows]
                acc[n, part, :, 128:256] += key_part[rows]
            keys = jnp.concatenate([kv[n, part, :, 128:256] for n, part, slot in chunks], axis=0)
            dq_t[high] += dot_tn(keys, grad_s)
            return carry

        return grads

    def d_copy(part, half):
        return remote(
            sd.at[part, half], rd.at[part, half], d_s.at[part, half], d_r.at[part, half], c_dev
        )

    def split(part, half):
        def step(n, carry):
            for h in (0, 1):
                rows = pl.ds(pl.multiple_of((2 * h + 1 - core) * 32, 32), 32)
                sd[part, half, n, h] = acc[4 * half + n, part, rows, :].astype(BF)
            return carry

        lax.fori_loop(0, 4, step, 0, unroll=True)
        d_copy(part, half).start()

    def xx_copy(part, half, k):
        return remote(
            sx.at[part, half, (x + k) % 4], rx.at[part, half, k],
            xx_s.at[part, half, k], xx_r.at[part, half, k], x_dev(k),
        )

    def sum_cores(part, half):
        d_copy(part, half).wait()

        def step(n, carry):
            for h in (0, 1):
                rows = pl.ds(pl.multiple_of((2 * h + core) * 32, 32), 32)
                both = acc[4 * half + n, part, rows, :] + rd[part, half, n, h].astype(F32)
                both = both.astype(BF)
                sx[part, half, h, n] = both[0:16]
                sx[part, half, 2 + h, n] = both[16:32]
            return carry

        lax.fori_loop(0, 4, step, 0, unroll=True)
        for k in (2, 1, 3):
            xx_copy(part, half, k).start()

    def zz_copy(part, k):
        return remote(
            sz.at[part, (z + k) % 8], rz.at[part, k], zz_s.at[part, k], zz_r.at[part, k], z_dev(k)
        )

    def meets(part, source, target):
        return (target >= source) if part else ((target <= source) | (target >= 7 - source))

    def sum_x(part, half):
        for k in (1, 3, 2):
            xx_copy(part, half, k).wait()

        def step(n, carry):
            total = sx[part, half, x, n].astype(F32)
            total += sum(rx[part, half, k, n].astype(F32) for k in (1, 2, 3))
            sz[part, 4 * half + n] = total.astype(BF)
            return carry

        lax.fori_loop(0, 4, step, 0, unroll=True)
        for k in (4, 3, 5, 2, 6, 1, 7):
            target = (z + k) % 8

            @pl.when((target // 4 == half) & meets(part, z, target))
            def _():
                zz_copy(part, k).start()

    def h_copy(part, k):
        mine = fin.at[part, pl.ds(own_rows, 16), :]
        return remote(mine, mine, h_s.at[part, k], h_r.at[part, k], h_dev(k))

    def sum_z(part):
        for k in (1, 7, 2, 6, 3, 5, 4):

            @pl.when(meets(part, (z + 8 - k) % 8, z))
            def _():
                zz_copy(part, k).wait_recv()

        total = sz[part, z].astype(F32) + sum(rz[part, k].astype(F32) for k in range(1, 8))
        total = jnp.concatenate([total[:, 0:128], total[:, 128:256] * SCALE], axis=1)
        fin[part, pl.ds(own_rows, 16), :] = total.astype(BF)
        for k in (6, 2, 4, 1, 3, 5, 7):
            h_copy(part, k).start()

    def stores(part):
        rows = pl.ds(128 * part, 128)
        return [
            pltpu.make_async_copy(fin.at[part, :, pl.ds(0, 128)], gv_ref.at[rows, :], o_s.at[part, 0]),
            pltpu.make_async_copy(fin.at[part, :, pl.ds(128, 128)], gk_ref.at[rows, :], o_s.at[part, 1]),
        ]

    def gathered(part):
        for k in (4, 1, 7, 3, 5, 2, 6):
            sender = (head + 8 - k) % 8
            rows = pl.multiple_of((sender % 4) * 32 + (sender // 4) * 16, 16)
            theirs = fin.at[part, pl.ds(rows, 16), :]
            remote(theirs, theirs, h_s.at[part, k], h_r.at[part, k], h_dev(k)).wait_recv()
        for copy in stores(part):
            copy.start()

    dq_t[...] = jnp.zeros((2, 128, 512), F32)
    high_grads = grads_of(1, *row_stats(1))
    lax.fori_loop(0, 1, high_grads, 0)
    split(1, 1)

    @pl.when(z < 4)
    def _():
        split(1, 0)

    def turn(high):
        for a in range(4):
            rows = slice(128 * high, 128 * high + 128)
            sq[a, rows, :] = dq_t[high, :, 128 * a : 128 * a + 128].T.astype(BF)

    turn(1)
    low_grads = grads_of(0, *row_stats(0))
    sum_cores(1, 1)
    low_grads(0, 0)
    split(0, 0)

    @pl.when(z < 4)
    def _():
        sum_cores(1, 0)

    @pl.when(z >= 4)
    def _():
        low_grads(1, 0)

    split(0, 1)

    sum_cores(0, 0)
    turn(0)
    sum_cores(0, 1)
    q_copies = []
    for k in (2, 1, 3):
        copy = remote(sq.at[(y + k) % 4], rq.at[k], q_s.at[k], q_r.at[k], y_dev(k))
        copy.start()
        q_copies.append(copy)
    sum_x(1, 1)

    @pl.when(z < 4)
    def _():
        sum_x(1, 0)

    sum_x(0, 0)
    sum_x(0, 1)
    for copy in q_copies:
        copy.wait()
    total = sq[y].astype(F32) + sum(rq[k].astype(F32) for k in (1, 2, 3))
    gq[...] = (SCALE * total).astype(BF)
    gq_store = pltpu.make_async_copy(gq, gq_ref, o_s.at[2, 0])
    gq_store.start()
    send_waits()
    sum_z(1)
    sum_z(0)
    gathered(1)
    gathered(0)
    for part in (1, 0):
        for k in range(1, 8):
            h_copy(part, k).wait_send()

            @pl.when(meets(part, z, (z + k) % 8))
            def _():
                zz_copy(part, k).wait_send()

        for copy in stores(part):
            copy.wait()
    gq_store.wait()


def write_out(a, b, c, a_out, b_out, c_out, a_mid, b_mid, c_mid, sems):
    mids = (a_mid, b_mid, c_mid)
    first = [pltpu.make_async_copy(r, m, sems.at[n, 0]) for n, (r, m) in enumerate(zip((a, b, c), mids))]
    last = [pltpu.make_async_copy(m, r, sems.at[n, 1]) for n, (r, m) in enumerate(zip((a_out, b_out, c_out), mids))]
    for copy in first:
        copy.start()
    for one, two in zip(first, last):
        one.wait()
        two.start()
    for copy in last:
        copy.wait()


def body(query, key, value, grad_out, doc_ids, tile_mask):
    hbm = pl.BlockSpec(memory_space=pltpu.HBM)
    dma = lambda *shape: pltpu.SemaphoreType.DMA(shape)
    scratch = [
        pltpu.VMEM((8, 2, 128, 256), BF),
        pltpu.VMEM((8, 2, 128, 128), BF),
        pltpu.VMEM((2, 4, 128, 256), BF),
        pltpu.VMEM((2, 128, 128), BF),
        pltpu.VMEM((64, 128), jnp.int32),
        pltpu.VMEM((64, 64), jnp.int32),
        pltpu.VMEM((128, 128), F32),
        pltpu.VMEM((8, 128), F32),
        pltpu.VMEM((24, 128, 512), F32),
        pltpu.VMEM((24, 128, 512), F32),
        pltpu.VMEM((24, 4, 8, 128), F32),
        pltpu.VMEM((24, 4, 8, 128), F32),
        pltpu.VMEM((24, 4, 8, 128), F32),
        pltpu.VMEM((2, 16, 128), F32),
        pltpu.VMEM((4, 2, 16, 128), F32),
        pltpu.VMEM((8, 2, 128, 256), F32),
        pltpu.VMEM((2, 128, 512), F32),
        pltpu.VMEM((4, 256, 128), BF),
        pltpu.VMEM((4, 256, 128), BF),
        pltpu.VMEM((2, 2, 4, 2, 32, 256), BF),
        pltpu.VMEM((2, 2, 4, 2, 32, 256), BF),
        pltpu.VMEM((2, 2, 4, 4, 16, 256), BF),
        pltpu.VMEM((2, 2, 4, 4, 16, 256), BF),
        pltpu.VMEM((2, 8, 16, 256), BF),
        pltpu.VMEM((2, 8, 16, 256), BF),
        pltpu.VMEM((2, 128, 256), BF),
        pltpu.VMEM((256, 128), BF),
        dma(3, 2),
        dma(10), dma(8, 2), dma(8, 2), dma(4), dma(4), dma(4, 8, 2), dma(4, 8, 2), dma(4), dma(4),
        dma(2, 4), dma(2, 4), dma(4), dma(4),
        dma(2, 2), dma(2, 2), dma(2, 2, 4), dma(2, 2, 4), dma(2, 8), dma(2, 8), dma(2, 8), dma(2, 8),
    ]
    grad_query, grad_key, grad_value = pl.pallas_call(
        kernel,
        out_shape=[jax.ShapeDtypeStruct((256, 128), BF)] * 3,
        in_specs=[hbm] * 6,
        out_specs=[hbm] * 3,
        scratch_shapes=scratch,
        compiler_params=pltpu.CompilerParams(
            collective_id=0, has_side_effects=True, vmem_limit_bytes=56 << 20
        ),
        cost_estimate=pl.CostEstimate(flops=3 << 30, bytes_accessed=1 << 20, transcendentals=1 << 20),
        name="attention_grads",
    )(
        query.reshape(256, 128),
        grad_out.reshape(256, 128),
        key,
        value,
        doc_ids.reshape(64, 128),
        tile_mask,
    )
    grad_query, grad_key, grad_value = pl.pallas_call(
        write_out,
        out_shape=[jax.ShapeDtypeStruct((256, 128), BF)] * 3,
        in_specs=[hbm] * 3,
        out_specs=[hbm] * 3,
        scratch_shapes=[pltpu.VMEM((256, 128), BF)] * 3 + [dma(3, 2)],
        compiler_params=pltpu.CompilerParams(vmem_limit_bytes=56 << 20),
        name="write_out",
    )(grad_query, grad_key, grad_value)
    return grad_query.reshape(256, 1, 128), grad_key, grad_value


def solution(mesh):
    rows, heads = P("ctx", None), P("ctx", "head", None)
    return jax.shard_map(
        body,
        mesh=mesh,
        in_specs=(heads, rows, rows, heads, P(), P()),
        out_specs=(heads, rows, rows),
        check_vma=False,
    )
```
